512 devices in a mesh: section: 4 (over z_hi), vocab: 32 (over z_lo, y, core), dp: 4 (over x).
Axes of the slice: x: 4, y: 4, z: 16 (z_hi: 4, z_lo: 4; z = z_hi * 4 + z_lo), core: 2. Of those that a mesh axis runs over, the one named last changes fastest.
Arguments:
- features: bfloat16 [4, 128, 32, 3072], P('dp', 'vocab', None, 'section'), may hold values from -6 to 6
- dw_weight: float32 [7, 7, 3072], P(None, None, 'section'), may hold values from -1.75 to 1.75
- ln_gain: float32 [3072], P('section'), may hold values from 0.25 to 1.75
- ln_bias: float32 [3072], P('section'), may hold values from -3 to 3
- layer_scale: float32 [3072], P('section'), may hold values from 0.25 to 2
- proj_weight: bfloat16 [3072, 8192], P('section', 'vocab'), may hold values from -0.109375 to 0.109375
- text_embed: bfloat16 [4, 512, 8192], P('dp', 'section', 'vocab'), may hold values from -6 to 6
- positions: int32 [4, 256], P('dp'), may hold values from 0 to 511, as said below
- rms_gain: float32 [8192], replicated, may hold values from 0.25 to 1.75
- head_weight: bfloat16 [8192, 64128], P('dp', ('section', 'vocab'))
- labels: int32 [4, 512], P('dp'), may hold values from 0 to 64127
Outputs:
- visual: bfloat16 [4, 256, 3072], P('dp', 'vocab', 'section')
- loss: float32 [4, 512], P('dp', 'section')
The draws below stay inside these ranges and needn't reach their ends.
Inputs may be any that keep to these rules, and one draw needn't show every extreme that they name: The positions of one sequence are distinct.
All inputs are finite; a program needn't handle non-finite values.
Results may differ from the reference program's by a relative error of at most 0.008.
Values may be sent and summed in bfloat16 or wider, within the bound.
No kernel may reach another device: no remote copies, remote signals or barrier semaphores. Data moves between devices by JAX's collectives and lax.ppermute only.
A program may use at most 64 MiB of HBM per device.

```python
import math
import jax
import jax.numpy as jnp
import numpy as np
from jax import lax

C = 3072
D = 8192
COLS = 32
BATCH = 4
ROWS = 128
NV = 256
SEQ = 512
VOCAB = 64128


def draw_positions(key, part):
    key = jax.random.fold_in(key, 5)
    keys = jax.random.split(key, BATCH)
    picks = jax.vmap(lambda one: jax.random.permutation(one, SEQ)[:NV])(keys)
    return picks.astype(jnp.int32)


def draw_head_weight(key, part):
    key = jax.random.fold_in(key, 11)
    first, second = jax.random.split(key)
    base = jax.random.normal(first, (D, VOCAB), jnp.float32) * D ** (-0.5)
    scales = jnp.exp(jax.random.uniform(second, (1, VOCAB), jnp.float32, 0.0, math.log(4.0)))
    return (base * scales).astype(jnp.bfloat16)


def plant(values, key, smallest, top_value):
    index_at = [jax.random.randint(jax.random.fold_in(key, axis), (), 0, length) for axis, length in enumerate(values.shape)]
    main_axis = values.shape.index(max(values.shape))
    neighbour = index_at[:main_axis] + [(index_at[main_axis] + 1) % values.shape[main_axis]] + index_at[main_axis + 1:]
    return values.at[tuple(index_at)].set(smallest).at[tuple(neighbour)].set(top_value)


def level_of(rng, dims, shards, least, top_value):
    loudness = 1.0
    for axis_at, blocks in shards:
        draws = jax.random.uniform(jax.random.fold_in(jax.random.fold_in(rng, 6), axis_at), (blocks,), jnp.float32, least / len(shards), top_value / len(shards))
        loudness = loudness * jnp.repeat(jnp.exp(draws), dims[axis_at] // blocks).reshape((-1,) + (1,) * (len(dims) - 1 - axis_at))
    return loudness


def cumulative_ranks(count, lean):
    portions = [(1 << 20) // math.isqrt(grade ** lean) + 1 for grade in range(1, count + 1)]
    scale = 1 + sum(portions) // (1 << 30)
    return np.cumsum(np.array([max(1, weight // scale) for weight in portions]))


def skewed_ids(rng, extent, number_of, skew):
    table = cumulative_ranks(number_of, skew)
    lot = jax.random.randint(jax.random.fold_in(rng, 1), extent, 0, int(table[number_of - 1]))
    standing = jnp.searchsorted(jnp.asarray(table, jnp.int32), lot, side="right")
    return jax.random.permutation(jax.random.fold_in(rng, 2), number_of)[standing].astype(jnp.int32)


def noise(stream_key, shape, scale, bound, cuts=(), held_as=jnp.bfloat16):
    drawn = jax.random.normal(stream_key, shape, jnp.float32) * scale
    if len(cuts) > 0:
        drawn = level_of(stream_key, shape, cuts, -0.22, 0.18) * drawn
    return jnp.clip(drawn, min=-bound, max=bound).astype(held_as)


def setup_inputs(seed: int = 0) -> dict:
    seeds = jax.random.split(jax.random.key(seed), 12)
    features = noise(seeds[0], (BATCH, ROWS, COLS, C), 1.0, 6.0, ((0, 4), (1, 32), (3, 4)))
    dw_weight = noise(seeds[1], (7, 7, C), 12 ** -0.5, 1.75, ((2, 4),), jnp.float32)
    ln_gain = jnp.clip(1.0 + 0.15 * jax.random.normal(seeds[2], (C,), jnp.float32), 0.25, 1.75)
    ln_bias = noise(seeds[3], (C,), 0.5, 3.0, ((0, 4),), jnp.float32)
    layer_scale = jnp.clip(jnp.exp(math.log(2.0) - 2.0794415 * jax.random.uniform(seeds[4], (C,), jnp.float32) ** level_of(seeds[4], (C,), ((0, 4),), -0.2, 0.2)), 0.25, 2.0)
    proj_weight = noise(seeds[5], (C, D), C ** -0.5, 0.109375, ((0, 4), (1, 32)))
    text_embed = noise(seeds[6], (BATCH, SEQ, D), 1.0, 6.0, ((0, 4), (1, 4), (2, 32)))
    positions = draw_positions(jax.random.fold_in(seeds[11], 71), 0)
    rms_gain = jnp.clip(1.0 + 0.15 * jax.random.normal(seeds[8], (D,), jnp.float32), 0.25, 1.75)
    head_weight = draw_head_weight(jax.random.fold_in(seeds[11], 71), 0)
    labels = plant(skewed_ids(seeds[10], (BATCH, SEQ), VOCAB, 2), jax.random.fold_in(seeds[10], 3), 0, VOCAB - 1).astype(jnp.int32)
    return {"features": features, "dw_weight": dw_weight, "ln_gain": ln_gain, "ln_bias": ln_bias, "layer_scale": layer_scale, "proj_weight": proj_weight, "text_embed": text_embed, "positions": positions, "rms_gain": rms_gain, "head_weight": head_weight, "labels": labels}


def depthwise(image, dw_weight):
    height = image.shape[0]
    width = image.shape[1]
    padded = jnp.pad(image.astype(jnp.float32), ((3, 3), (3, 3), (0, 0)))
    total = jnp.zeros(image.shape, jnp.float32)
    for row_off in range(7):
        for col_off in range(7):
            total = total + padded[row_off:row_off + height, col_off:col_off + width] * dw_weight[row_off, col_off]
    return total

def one_sample(image, text, places, targets, dw_weight, ln_gain, ln_bias, layer_scale, proj_weight, rms_gain, head_weight):
    conv = depthwise(image, dw_weight)
    middle = lax.optimization_barrier(jnp.mean(conv, axis=-1, keepdims=True))
    spread = lax.optimization_barrier(jnp.mean(jnp.square(conv - middle), axis=-1, keepdims=True))
    normal = (conv - middle) * lax.rsqrt(spread + 1e-06) * ln_gain + ln_bias
    block = image.astype(jnp.float32) + layer_scale * normal
    height, width, chans = block.shape
    pooled = block.reshape(height // 4, 4, width // 4, 4, chans).mean(axis=(1, 3))
    pooled = pooled.reshape(-1, chans).astype(jnp.bfloat16)
    projected = jnp.dot(pooled, proj_weight, preferred_element_type=jnp.float32).astype(jnp.bfloat16)
    sequence = text.at[places].set(projected)
    wide = sequence.astype(jnp.float32)
    normed = (wide * lax.rsqrt(lax.optimization_barrier(jnp.mean(wide * wide, axis=-1, keepdims=True)) + 1e-05) * rms_gain).astype(jnp.bfloat16)
    logits = jnp.dot(normed, head_weight, preferred_element_type=jnp.float32)
    top = lax.optimization_barrier(jnp.max(logits, axis=-1))
    total = lax.optimization_barrier(jnp.sum(jnp.exp(logits - top[:, None]), axis=-1))
    chosen = jnp.take_along_axis(logits, targets[:, None].astype(jnp.int32), axis=1)[:, 0]
    return (pooled, top + jnp.log(total) - chosen)

def reference(features, dw_weight, ln_gain, ln_bias, layer_scale, proj_weight, text_embed, positions, rms_gain, head_weight, labels):

    def step(items):
        image, text, places, targets = items
        return one_sample(image, text, places, targets, dw_weight, ln_gain, ln_bias, layer_scale, proj_weight, rms_gain, head_weight)
    visual, loss = lax.map(step, (features, text_embed, positions, labels))
    return (visual, loss)
```

```python
import functools

import jax
import jax.numpy as jnp
from jax import lax
from jax.experimental import pallas as pl
from jax.experimental.pallas import tpu as pltpu
from jax.sharding import PartitionSpec as P

WIDE = 256


def shifted(value, axis, step):
    count = lax.axis_size(axis)
    return lax.ppermute(value, axis, [((i + step) % count, i) for i in range(count)])


def extended(cells, axis, width):
    count = lax.axis_size(axis)
    ends = count - 1
    head, tail = cells[:width], cells[-width:]
    return jnp.concatenate(
        [
            lax.ppermute(tail, axis, [(i, (i + 1) % count) for i in range(ends)]),
            cells,
            lax.ppermute(head, axis, [((i + 1) % count, i) for i in range(ends)]),
        ],
        axis=0,
    )


def head_kernel(
    columns,
    offsets,
    own_ref,
    gain_ref,
    slots_ref,
    ids_ref,
    x_any,
    dep_any,
    *refs,
):
    w_any, out_ref = refs[:8], refs[8]
    x_v, w_v, first, second, squares, sem_x, sem_w = refs[9:]
    parts, rows, depth = x_v.shape
    own = own_ref[0]

    def x_copy(j):
        block = lax.rem(own + offsets[j], parts)
        start = pl.multiple_of(block * depth, depth)
        return pltpu.make_async_copy(
            x_any.at[:, pl.ds(start, depth)], x_v.at[j], sem_x.at[j]
        )

    def w_copy(i):
        return pltpu.make_async_copy(w_any[i], w_v.at[i], sem_w.at[i])

    for j in range(parts):
        x_copy(j).start()
        w_copy(2 * j).start()
        w_copy(2 * j + 1).start()
    for j in range(parts):
        x_copy(j).wait()
        wide = x_v[j].astype(jnp.float32)
        sums = jnp.sum(wide * wide, axis=1, keepdims=True)
        gain = gain_ref[lax.rem(own + offsets[j], parts)]
        scaled = (wide * gain).astype(jnp.bfloat16)
        for half, total in enumerate((first, second)):
            w_copy(2 * j + half).wait()
            part = lax.dot_general(
                scaled,
                w_v[2 * j + half],
                (((1,), (1,)), ((), ())),
                preferred_element_type=jnp.float32,
            )
            if j == 0:
                total[...] = part
            else:
                total[...] += part
        if j == 0:
            squares[...] = sums
        else:
            squares[...] += sums
    factor = lax.rsqrt(squares[...] / (parts * depth) + 1e-05)
    low = first[...] * factor
    high = second[...] * factor
    ids = ids_ref[...]
    low_at = lax.broadcasted_iota(jnp.int32, low.shape, 1)
    high_at = low_at + low.shape[1]
    real = high_at < columns
    high = jnp.where(real, high, -jnp.inf)
    top = jnp.maximum(
        jnp.max(low, axis=1, keepdims=True), jnp.max(high, axis=1, keepdims=True)
    )
    total = jnp.sum(jnp.exp(low - top), axis=1, keepdims=True) + jnp.sum(
        jnp.exp(high - top), axis=1, keepdims=True
    )
    chosen = jnp.sum(jnp.where(low_at == ids, low, 0.0), axis=1, keepdims=True) + jnp.sum(
        jnp.where((high_at == ids) & real, high, 0.0), axis=1, keepdims=True
    )
    places = out_ref.shape[1]
    hit = lax.broadcasted_iota(jnp.int32, (rows, places), 1) == slots_ref[...]
    out_ref[...] = jnp.zeros(out_ref.shape, jnp.float32)
    for at, value in enumerate((top, total, chosen)):
        out_ref[at : at + 1, :] = jnp.sum(
            jnp.where(hit, value, 0.0), axis=0, keepdims=True
        )


def head_stats(own, gain, slots, ids, x, dep, weights, columns, offsets, places):
    rows, width = x.shape
    parts = len(offsets)
    depth = width // parts
    vmem = pl.BlockSpec(memory_space=pltpu.VMEM)
    anywhere = pl.BlockSpec(memory_space=pl.ANY)
    return pl.pallas_call(
        functools.partial(head_kernel, columns, offsets),
        out_shape=jax.ShapeDtypeStruct((8, places), jnp.float32),
        in_specs=[pl.BlockSpec(memory_space=pltpu.SMEM), vmem, vmem, vmem]
        + [anywhere] * (2 + len(weights)),
        out_specs=vmem,
        scratch_shapes=[
            pltpu.VMEM((parts, rows, depth), jnp.bfloat16),
            pltpu.VMEM((2 * parts, WIDE, depth), jnp.bfloat16),
            pltpu.VMEM((rows, WIDE), jnp.float32),
            pltpu.VMEM((rows, WIDE), jnp.float32),
            pltpu.VMEM((rows, 1), jnp.float32),
            pltpu.SemaphoreType.DMA((parts,)),
            pltpu.SemaphoreType.DMA((2 * parts,)),
        ],
        compiler_params=pltpu.CompilerParams(vmem_limit_bytes=40 * 1024 * 1024),
        cost_estimate=pl.CostEstimate(
            flops=4 * rows * WIDE * width,
            bytes_accessed=2 * width * (rows + 2 * WIDE),
            transcendentals=2 * rows * WIDE,
        ),
    )(own, gain, slots, ids, x, dep, *weights)


def shards(
    features,
    dw_weight,
    ln_gain,
    ln_bias,
    layer_scale,
    proj_weight,
    text_embed,
    positions,
    rms_gain,
    head_weight,
    labels,
):
    sections = lax.axis_size("section")
    runs = lax.axis_size("vocab")
    parts = lax.axis_size("dp")
    section = lax.axis_index("section")
    shard_index = lax.axis_index(("section", "vocab"))
    places = positions[0]
    targets = labels[0]
    visual_rows = places.shape[0]
    places_all = targets.shape[0]
    text_rows = places_all - visual_rows
    columns = head_weight.shape[1]

    weight = head_weight.T
    low = weight[:WIDE]
    high = jnp.pad(weight[WIDE:], ((0, 2 * WIDE - columns), (0, 0)))
    low_left, high_right = shifted(low, "dp", -1), shifted(high, "dp", 1)
    high_left, low_right = shifted(high, "dp", -1), shifted(low, "dp", 1)

    image = features[0]
    height, width, chans = image.shape
    padded = extended(image, "vocab", 3)
    padded = jnp.pad(padded, ((0, 0), (3, 3), (0, 0))).astype(jnp.float32)
    conv = jnp.zeros((height, width, chans), jnp.float32)
    for row_off in range(7):
        for col_off in range(7):
            conv = (
                conv
                + padded[row_off : row_off + height, col_off : col_off + width]
                * dw_weight[row_off, col_off]
            )
    sums = jnp.stack(
        [jnp.sum(conv, axis=-1).reshape(-1), jnp.sum(conv * conv, axis=-1).reshape(-1)]
    )
    others = [shifted(sums, "section", step) for step in range(1, sections)]
    sums = sums + sum(others)
    all_chans = chans * sections
    middle = sums[0].reshape(height, width) / all_chans
    spread = sums[1].reshape(height, width) / all_chans - middle * middle
    normal = (conv - middle[..., None]) * lax.rsqrt(spread + 1e-06)[..., None] * ln_gain + ln_bias
    block = image.astype(jnp.float32) + layer_scale * normal
    pooled = block.reshape(height // 4, 4, width // 4, 4, chans).mean(axis=(1, 3))
    pooled = pooled.reshape(-1, chans).astype(jnp.bfloat16)

    tokens = lax.all_to_all(
        jnp.broadcast_to(pooled[None], (runs,) + pooled.shape), "vocab", 0, 0
    ).reshape(-1, chans)

    low_left_on, high_right_on, tokens = lax.optimization_barrier(
        (low_left, high_right, tokens)
    )
    low_far, high_far = shifted(low_left_on, "dp", -1), shifted(high_right_on, "dp", 1)

    partial = jnp.dot(tokens, proj_weight, preferred_element_type=jnp.float32)
    partial = partial.reshape(sections, -1, partial.shape[1])
    owned = lax.dynamic_index_in_dim(partial, section, 0, keepdims=False)
    for step in range(1, sections):
        out = lax.dynamic_index_in_dim(
            partial, lax.rem(section + step, sections), 0, keepdims=False
        ).astype(jnp.bfloat16)
        owned = owned + shifted(out, "section", -step).astype(jnp.float32)
    owned = owned.astype(jnp.bfloat16)
    projected = jnp.concatenate(
        [owned] + [shifted(owned, "section", step) for step in range(1, sections)]
    )
    visual_slots = lax.dynamic_slice_in_dim(
        jnp.concatenate([places, places]),
        section * (visual_rows // sections),
        visual_rows,
        0,
    )

    text = text_embed[0]
    text = jnp.concatenate(
        [text] + [shifted(text, "section", step) for step in range(1, sections)]
    )
    slots = lax.iota(jnp.int32, places_all)
    near = lax.rem(section * text_embed.shape[1] + slots, places_all)
    is_text = jnp.all(near[:, None] != places[None, :], axis=1)
    rank = jnp.sum(
        jnp.where((slots[None, :] < slots[:, None]) & is_text[None, :], 1, 0), axis=1
    )
    select = (rank[None, :] == lax.iota(jnp.int32, text_rows)[:, None]) & is_text[None, :]
    text = jnp.dot(
        select.astype(jnp.bfloat16), text, preferred_element_type=jnp.float32
    ).astype(jnp.bfloat16)
    text_slots = jnp.sum(jnp.where(select, near[None, :], 0), axis=1)
    text_all = lax.all_gather(text, "vocab", axis=1, tiled=True)
    visual_all = lax.all_gather(projected, "vocab", axis=1, tiled=True)

    gain = rms_gain.reshape(parts, 1, -1)
    own = lax.axis_index("dp").reshape(1)
    weights = (
        low,
        high,
        low_left,
        high_left,
        low_right,
        high_right,
        low_far,
        high_far,
    )
    offsets = (0, parts - 1, 1, 2)

    def stats(at, rows, dep):
        ids = jnp.sum(jnp.where(at[:, None] == slots[None, :], targets[None, :], 0), axis=1)
        ids = ids - shard_index * columns
        return head_stats(
            own, gain, at[:, None], ids[:, None], rows, dep, weights, columns, offsets, places_all
        )

    of_text = stats(text_slots, text_all, projected)
    of_visual = stats(visual_slots, visual_all, of_text)
    both = (of_text + of_visual)[:3].reshape(3, sections, -1).transpose(1, 0, 2)
    both = jnp.broadcast_to(both[:, None], (sections, runs) + both.shape[1:])
    both = both.reshape((sections * runs,) + both.shape[2:])
    every = lax.all_to_all(both, ("section", "vocab"), 0, 0)
    tops, totals, chosen = every[:, 0], every[:, 1], every[:, 2]
    top = jnp.max(tops, axis=0)
    total = jnp.sum(totals * jnp.exp(tops - top), axis=0)
    loss = top + jnp.log(total) - jnp.sum(chosen, axis=0)
    return (pooled[None], loss[None])


def solution(mesh):
    in_specs = (
        P("dp", "vocab", None, "section"),
        P(None, None, "section"),
        P("section"),
        P("section"),
        P("section"),
        P("section", "vocab"),
        P("dp", "section", "vocab"),
        P("dp", None),
        P(),
        P("dp", ("section", "vocab")),
        P("dp", None),
    )
    out_specs = (P("dp", "vocab", "section"), P("dp", "section"))
    return jax.shard_map(shards, mesh=mesh, in_specs=in_specs, out_specs=out_specs, check_vma=False)
```

```python
import functools

import jax
import jax.numpy as jnp
from jax import lax
from jax.experimental import pallas as pl
from jax.experimental.pallas import tpu as pltpu
from jax.sharding import PartitionSpec as P

WIDE = 256
VOCAB = ("zl", "y", "core")


def shifted(value, axis, step):
    count = lax.axis_size(axis)
    return lax.ppermute(value, axis, [((i + step) % count, i) for i in range(count)])


def extended(cells, axis, width):
    count = lax.axis_size(axis)
    ends = count - 1
    head, tail = cells[:width], cells[-width:]
    return jnp.concatenate(
        [
            lax.ppermute(tail, axis, [(i, (i + 1) % count) for i in range(ends)]),
            cells,
            lax.ppermute(head, axis, [((i + 1) % count, i) for i in range(ends)]),
        ],
        axis=0,
    )


def head_kernel(columns, offsets, from_text, own_ref, gain_ref, slots_ref, ids_ref, *refs):
    x_v, w_v, scaled, total, squares, sem_x, sem_w = refs[-7:]
    out_ref = refs[-8]
    w_own, w_left, w_right, w_low, w_high = refs[-13:-8]
    parts, lines, cores, rows, width = x_v.shape
    own, core = own_ref[0], own_ref[1]

    def block(j):
        return lax.rem(own + offsets[j], parts)

    def x_copies(j):
        if from_text:
            text = refs[0]
            size = text.shape[4]
            return [
                pltpu.make_async_copy(
                    text.at[k, block(j)],
                    x_v.at[j, :, :, pl.ds(k * size, size)],
                    sem_x.at[j, k],
                )
                for k in range(text.shape[0])
            ]
        return [
            pltpu.make_async_copy(
                refs[k].at[:, block(j)],
                x_v.at[j, :, core if k == 0 else 1 - core],
                sem_x.at[j, k],
            )
            for k in range(2)
        ]

    def w_copies(j):
        if j < 3:
            return [
                pltpu.make_async_copy((w_own, w_left, w_right)[j], w_v.at[j], sem_w.at[j])
            ]
        return [
            pltpu.make_async_copy(w_low, w_v.at[3, pl.ds(0, WIDE)], sem_w.at[3]),
            pltpu.make_async_copy(w_high, w_v.at[3, pl.ds(WIDE, WIDE)], sem_w.at[4]),
        ]

    for j in range(parts):
        for copy in x_copies(j) + w_copies(j):
            copy.start()
    for j in range(parts):
        for copy in x_copies(j):
            copy.wait()
        sums = jnp.zeros((rows, width), jnp.float32)
        for line in range(lines):
            for at in range(cores):
                piece = line * cores + at
                wide = x_v[j, line, at].astype(jnp.float32)
                sums = sums + wide * wide
                gain = gain_ref[block(j) * (lines * cores) + piece]
                scaled[:, piece * width : (piece + 1) * width] = (wide * gain).astype(
                    jnp.bfloat16
                )
        for copy in w_copies(j):
            copy.wait()
        part = lax.dot_general(
            scaled[...], w_v[j], (((1,), (1,)), ((), ())), preferred_element_type=jnp.float32
        )
        sums = jnp.sum(sums, axis=1, keepdims=True)
        if j == 0:
            total[...] = part
            squares[...] = sums
        else:
            total[...] += part
            squares[...] += sums
    factor = lax.rsqrt(squares[...] / (parts * lines * cores * width) + 1e-05)
    logits = total[...] * factor
    at = lax.broadcasted_iota(jnp.int32, logits.shape, 1)
    real = at < columns
    top = jnp.max(jnp.where(real, logits, -jnp.inf), axis=1, keepdims=True)
    summed = jnp.sum(
        jnp.where(real, jnp.exp(logits - top), 0.0), axis=1, keepdims=True
    )
    chosen = jnp.sum(
        jnp.where((at == ids_ref[...]) & real, logits, 0.0), axis=1, keepdims=True
    )
    hit = (
        lax.broadcasted_iota(jnp.int32, (rows, out_ref.shape[1]), 1) == slots_ref[...]
    )
    out_ref[...] = jnp.zeros(out_ref.shape, jnp.float32)
    for k, value in enumerate((top, summed, chosen)):
        out_ref[k : k + 1, :] = jnp.sum(jnp.where(hit, value, 0.0), axis=0, keepdims=True)


def head_stats(own, gain, slots, ids, xs, weights, dep, columns, offsets, places):
    from_text = len(xs) == 1
    rows = slots.shape[0]
    parts, lines, cores = len(offsets), 4, 2
    width = xs[0].shape[-1]
    depth = lines * cores * width
    vmem = pl.BlockSpec(memory_space=pltpu.VMEM)
    anywhere = pl.BlockSpec(memory_space=pl.ANY)
    return pl.pallas_call(
        functools.partial(head_kernel, columns, offsets, from_text),
        out_shape=jax.ShapeDtypeStruct((8, places), jnp.float32),
        in_specs=[pl.BlockSpec(memory_space=pltpu.SMEM), vmem, vmem, vmem]
        + [anywhere] * (len(xs) + len(dep) + len(weights)),
        out_specs=vmem,
        scratch_shapes=[
            pltpu.VMEM((parts, lines, cores, rows, width), jnp.bfloat16),
            pltpu.VMEM((parts, 2 * WIDE, depth), jnp.bfloat16),
            pltpu.VMEM((rows, depth), jnp.bfloat16),
            pltpu.VMEM((rows, 2 * WIDE), jnp.float32),
            pltpu.VMEM((rows, 1), jnp.float32),
            pltpu.SemaphoreType.DMA((parts, 4)),
            pltpu.SemaphoreType.DMA((parts + 1,)),
        ],
        compiler_params=pltpu.CompilerParams(vmem_limit_bytes=56 * 1024 * 1024),
        cost_estimate=pl.CostEstimate(
            flops=4 * rows * WIDE * parts * depth,
            bytes_accessed=2 * parts * depth * (rows + 2 * WIDE),
            transcendentals=2 * rows * WIDE,
        ),
    )(own, gain, slots, ids, *xs, *dep, *weights)


def to_all(value, axis):
    count = lax.axis_size(axis)
    return lax.all_to_all(jnp.broadcast_to(value[None], (count,) + value.shape), axis, 0, 0)


def shards(
    features,
    dw_weight,
    ln_gain,
    ln_bias,
    layer_scale,
    proj_weight,
    text_embed,
    positions,
    rms_gain,
    head_weight,
    labels,
):
    sections = lax.axis_size("section")
    parts = lax.axis_size("dp")
    shard_index = lax.axis_index(("section",) + VOCAB)
    places = positions[0]
    targets = labels[0]
    columns = head_weight.shape[1]
    slots = lax.iota(jnp.int32, targets.shape[0])

    text = text_embed[0]
    text_all = lax.all_gather(text, ("section",) + VOCAB, axis=0)
    text_all = text_all.reshape(
        (sections,) + tuple(lax.axis_size(axis) for axis in VOCAB) + text.shape
    )

    weight = jnp.pad(head_weight.T, ((0, 2 * WIDE - columns), (0, 0)))
    left, right = shifted(weight, "dp", -1), shifted(weight, "dp", 1)

    image = features[0]
    height, width, chans = image.shape
    padded = extended(image, VOCAB, 3)
    padded = jnp.pad(padded, ((0, 0), (3, 3), (0, 0))).astype(jnp.float32)
    conv = jnp.zeros((height, width, chans), jnp.float32)
    for row_off in range(7):
        for col_off in range(7):
            conv = (
                conv
                + padded[row_off : row_off + height, col_off : col_off + width]
                * dw_weight[row_off, col_off]
            )
    sums = jnp.stack(
        [jnp.sum(conv, axis=-1).reshape(-1), jnp.sum(conv * conv, axis=-1).reshape(-1)]
    )
    sums = jnp.sum(to_all(sums, "section"), axis=0)
    all_chans = chans * sections
    middle = sums[0].reshape(height, width) / all_chans
    spread = sums[1].reshape(height, width) / all_chans - middle * middle
    normal = (conv - middle[..., None]) * lax.rsqrt(spread + 1e-06)[..., None] * ln_gain + ln_bias
    block = image.astype(jnp.float32) + layer_scale * normal
    pooled = block.reshape(height // 4, 4, width // 4, 4, chans).mean(axis=(1, 3))
    pooled = pooled.reshape(-1, chans).astype(jnp.bfloat16)

    tokens = to_all(pooled, VOCAB).reshape(-1, chans)
    partial = jnp.dot(tokens, proj_weight, preferred_element_type=jnp.float32)
    partial = partial.astype(jnp.bfloat16).reshape(sections, -1, partial.shape[1])
    owned = lax.all_to_all(partial, "section", 0, 0).astype(jnp.float32)
    owned = jnp.sum(owned, axis=0).astype(jnp.bfloat16)

    rows = to_all(owned, "section").reshape(-1, owned.shape[1])
    rows = to_all(rows, "zl")
    rows, left, right = lax.optimization_barrier((rows, left, right))
    far_low, far_high = shifted(left[:WIDE], "dp", -1), shifted(right[WIDE:], "dp", 1)
    rows = to_all(rows, "y")
    rows, far_low, far_high = lax.optimization_barrier((rows, far_low, far_high))
    partner = lax.ppermute(rows, "core", [(0, 1), (1, 0)])

    gain = rms_gain.reshape(-1, 1, text.shape[1])
    own = jnp.stack([lax.axis_index("dp"), lax.axis_index("core")])
    offsets = (0, parts - 1, 1, 2)

    def stats(at, xs, dep):
        ids = jnp.sum(jnp.where(at[:, None] == slots[None, :], targets[None, :], 0), axis=1)
        ids = ids - shard_index * columns
        return head_stats(
            own,
            gain,
            at[:, None],
            ids[:, None],
            xs,
            (weight, left, right, far_low, far_high),
            dep,
            columns,
            offsets,
            targets.shape[0],
        )

    is_visual = jnp.any(slots[:, None] == places[None, :], axis=1)
    of_text = stats(jnp.where(is_visual, -1, slots), (text_all,), (rows[0, 0, :16, :128],))
    of_visual = stats(places, (rows, partner), ())
    both = (of_text + of_visual)[:3].reshape(3, sections, -1).transpose(1, 0, 2)

    def merged(parts_of):
        tops, totals, chosen = parts_of[:, 0], parts_of[:, 1], parts_of[:, 2]
        top = jnp.max(tops, axis=0)
        return jnp.stack(
            [top, jnp.sum(totals * jnp.exp(tops - top), axis=0), jnp.sum(chosen, axis=0)]
        )

    top, total, chosen = merged(to_all(merged(lax.all_to_all(both, "section", 0, 0)), VOCAB))
    loss = top + jnp.log(total) - chosen
    return (pooled[None], loss[None])


def solution(mesh):
    in_specs = (
        P("dp", VOCAB, None, "section"),
        P(None, None, "section"),
        P("section"),
        P("section"),
        P("section"),
        P("section", VOCAB),
        P("dp", "section", VOCAB),
        P("dp", None),
        P(),
        P("dp", ("section",) + VOCAB),
        P("dp", None),
    )
    out_specs = (P("dp", VOCAB, "section"), P("dp", "section"))
    sizes = (mesh.shape["section"], mesh.shape["vocab"] // 8, 4, 2, mesh.shape["dp"])
    mesh = jax.sharding.Mesh(mesh.devices.reshape(sizes), ("section",) + VOCAB + ("dp",))
    return jax.shard_map(shards, mesh=mesh, in_specs=in_specs, out_specs=out_specs, check_vma=False)
```

```python
import functools

import jax
import jax.numpy as jnp
from jax import lax
from jax.experimental import pallas as pl
from jax.experimental.pallas import tpu as pltpu
from jax.sharding import PartitionSpec as P

WIDE = 256
VOCAB = ("zl", "y", "core")


def shifted(value, axis, step):
    count = lax.axis_size(axis)
    return lax.ppermute(value, axis, [((i + step) % count, i) for i in range(count)])


def extended(cells, axis, width):
    count = lax.axis_size(axis)
    ends = count - 1
    head, tail = cells[:width], cells[-width:]
    return jnp.concatenate(
        [
            lax.ppermute(tail, axis, [(i, (i + 1) % count) for i in range(ends)]),
            cells,
            lax.ppermute(head, axis, [((i + 1) % count, i) for i in range(ends)]),
        ],
        axis=0,
    )


def head_kernel(columns, offsets, from_text, own_ref, gain_ref, slots_ref, ids_ref, *refs):
    x_v, w_v, scaled, total, squares, sem_x, sem_w = refs[-7:]
    out_ref = refs[-8]
    w_own, w_left, w_right, w_low, w_high = refs[-13:-8]
    parts, lines, cores, rows, width = x_v.shape
    own, core = own_ref[0], own_ref[1]

    def block(j):
        return lax.rem(own + offsets[j], parts)

    def x_copies(j):
        if from_text:
            return [pltpu.make_async_copy(refs[0].at[block(j)], x_v.at[j], sem_x.at[j, 0])]
        return [
            pltpu.make_async_copy(
                refs[k].at[:, block(j)],
                x_v.at[j, :, core if k == 0 else 1 - core],
                sem_x.at[j, k],
            )
            for k in range(2)
        ]

    def w_copies(j):
        if j < 3:
            return [
                pltpu.make_async_copy((w_own, w_left, w_right)[j], w_v.at[j], sem_w.at[j])
            ]
        return [
            pltpu.make_async_copy(w_low, w_v.at[3, pl.ds(0, WIDE)], sem_w.at[3]),
            pltpu.make_async_copy(w_high, w_v.at[3, pl.ds(WIDE, WIDE)], sem_w.at[4]),
        ]

    for j in range(parts):
        for copy in x_copies(j) + w_copies(j):
            copy.start()
    for j in range(parts):
        for copy in x_copies(j):
            copy.wait()
        sums = jnp.zeros((rows, width), jnp.float32)
        for line in range(lines):
            for at in range(cores):
                piece = line * cores + at
                wide = x_v[j, line, at].astype(jnp.float32)
                sums = sums + wide * wide
                gain = gain_ref[block(j) * (lines * cores) + piece]
                scaled[:, piece * width : (piece + 1) * width] = (wide * gain).astype(
                    jnp.bfloat16
                )
        for copy in w_copies(j):
            copy.wait()
        part = lax.dot_general(
            scaled[...], w_v[j], (((1,), (1,)), ((), ())), preferred_element_type=jnp.float32
        )
        sums = jnp.sum(sums, axis=1, keepdims=True)
        if j == 0:
            total[...] = part
            squares[...] = sums
        else:
            total[...] += part
            squares[...] += sums
    factor = lax.rsqrt(squares[...] / (parts * lines * cores * width) + 1e-05)
    logits = total[...] * factor
    at = lax.broadcasted_iota(jnp.int32, logits.shape, 1)
    real = at < columns
    top = jnp.max(jnp.where(real, logits, -jnp.inf), axis=1, keepdims=True)
    summed = jnp.sum(
        jnp.where(real, jnp.exp(logits - top), 0.0), axis=1, keepdims=True
    )
    chosen = jnp.sum(
        jnp.where((at == ids_ref[...]) & real, logits, 0.0), axis=1, keepdims=True
    )
    hit = (
        lax.broadcasted_iota(jnp.int32, (rows, out_ref.shape[1]), 1) == slots_ref[...]
    )
    out_ref[...] = jnp.zeros(out_ref.shape, jnp.float32)
    for k, value in enumerate((top, summed, chosen)):
        out_ref[k : k + 1, :] = jnp.sum(jnp.where(hit, value, 0.0), axis=0, keepdims=True)


def head_stats(own, gain, slots, ids, xs, weights, dep, columns, offsets, places):
    from_text = len(xs) == 1
    rows = slots.shape[0]
    parts, lines, cores = len(offsets), 4, 2
    width = xs[0].shape[-1]
    depth = lines * cores * width
    vmem = pl.BlockSpec(memory_space=pltpu.VMEM)
    anywhere = pl.BlockSpec(memory_space=pl.ANY)
    return pl.pallas_call(
        functools.partial(head_kernel, columns, offsets, from_text),
        out_shape=jax.ShapeDtypeStruct((8, places), jnp.float32),
        in_specs=[pl.BlockSpec(memory_space=pltpu.SMEM), vmem, vmem, vmem]
        + [anywhere] * (len(xs) + len(dep) + len(weights)),
        out_specs=vmem,
        scratch_shapes=[
            pltpu.VMEM((parts, lines, cores, rows, width), jnp.bfloat16),
            pltpu.VMEM((parts, 2 * WIDE, depth), jnp.bfloat16),
            pltpu.VMEM((rows, depth), jnp.bfloat16),
            pltpu.VMEM((rows, 2 * WIDE), jnp.float32),
            pltpu.VMEM((rows, 1), jnp.float32),
            pltpu.SemaphoreType.DMA((parts, 2)),
            pltpu.SemaphoreType.DMA((parts + 1,)),
        ],
        compiler_params=pltpu.CompilerParams(vmem_limit_bytes=56 * 1024 * 1024),
        cost_estimate=pl.CostEstimate(
            flops=4 * rows * WIDE * parts * depth,
            bytes_accessed=2 * parts * depth * (rows + 2 * WIDE),
            transcendentals=2 * rows * WIDE,
        ),
    )(own, gain, slots, ids, *xs, *dep, *weights)


def across(value, turn):
    count = lax.axis_size("section")
    pairs = [(i, i ^ 1) if turn == 0 else (i, count - 1 - i) for i in range(count)]
    return lax.ppermute(value, "section", pairs)


def to_all(value, axis):
    count = lax.axis_size(axis)
    return lax.all_to_all(jnp.broadcast_to(value[None], (count,) + value.shape), axis, 0, 0)


def shards(
    features,
    dw_weight,
    ln_gain,
    ln_bias,
    layer_scale,
    proj_weight,
    text_embed,
    positions,
    rms_gain,
    head_weight,
    labels,
):
    sections = lax.axis_size("section")
    parts = lax.axis_size("dp")
    shard_index = lax.axis_index(("section",) + VOCAB)
    places = positions[0]
    targets = labels[0]
    columns = head_weight.shape[1]
    slots = lax.iota(jnp.int32, targets.shape[0])

    text = to_all(text_embed[0], "section").reshape(slots.shape[0], -1)
    is_text = jnp.all(slots[:, None] != places[None, :], axis=1)
    rank = jnp.sum(
        jnp.where((slots[None, :] < slots[:, None]) & is_text[None, :], 1, 0), axis=1
    )
    text_rows = slots.shape[0] - places.shape[0]
    select = (rank[None, :] == lax.iota(jnp.int32, text_rows)[:, None]) & is_text[None, :]
    text = jnp.dot(
        select.astype(jnp.bfloat16), text, preferred_element_type=jnp.float32
    ).astype(jnp.bfloat16)
    text_slots = jnp.sum(jnp.where(select, slots[None, :], 0), axis=1)
    text_all = lax.all_gather(text, VOCAB, axis=0)
    text_all = text_all.reshape(tuple(lax.axis_size(axis) for axis in VOCAB) + text.shape)

    weight = jnp.pad(head_weight.T, ((0, 2 * WIDE - columns), (0, 0)))
    left, right = shifted(weight, "dp", -1), shifted(weight, "dp", 1)

    image = features[0]
    height, width, chans = image.shape
    padded = extended(image, VOCAB, 3)
    padded = jnp.pad(padded, ((0, 0), (3, 3), (0, 0))).astype(jnp.float32)
    conv = jnp.zeros((height, width, chans), jnp.float32)
    for row_off in range(7):
        for col_off in range(7):
            conv = (
                conv
                + padded[row_off : row_off + height, col_off : col_off + width]
                * dw_weight[row_off, col_off]
            )
    sums = jnp.stack(
        [jnp.sum(conv, axis=-1).reshape(-1), jnp.sum(conv * conv, axis=-1).reshape(-1)]
    )
    for turn in range(2):
        sums = sums + across(sums, turn)
    all_chans = chans * sections
    middle = sums[0].reshape(height, width) / all_chans
    spread = sums[1].reshape(height, width) / all_chans - middle * middle
    normal = (conv - middle[..., None]) * lax.rsqrt(spread + 1e-06)[..., None] * ln_gain + ln_bias
    block = image.astype(jnp.float32) + layer_scale * normal
    pooled = block.reshape(height // 4, 4, width // 4, 4, chans).mean(axis=(1, 3))
    pooled = pooled.reshape(-1, chans).astype(jnp.bfloat16)

    tokens = to_all(pooled, VOCAB).reshape(-1, chans)
    rows = jnp.dot(tokens, proj_weight, preferred_element_type=jnp.float32)
    for turn in range(2):
        rows = rows + across(rows.astype(jnp.bfloat16), turn).astype(jnp.float32)
    rows = rows.astype(jnp.bfloat16)

    rows, left, right = lax.optimization_barrier((rows, left, right))
    far_low, far_high = shifted(left[:WIDE], "dp", -1), shifted(right[WIDE:], "dp", 1)
    rows = to_all(rows, "zl")
    rows, text_all = lax.optimization_barrier((rows, text_all))
    early = rows[0, :16, :128]
    rows = to_all(rows, "y")
    rows, far_low, far_high = lax.optimization_barrier((rows, far_low, far_high))
    partner = lax.ppermute(rows, "core", [(0, 1), (1, 0)])

    gain = rms_gain.reshape(-1, 1, text.shape[1])
    own = jnp.stack([lax.axis_index("dp"), lax.axis_index("core")])
    offsets = (0, parts - 1, 1, 2)

    def stats(at, xs, dep):
        ids = jnp.sum(jnp.where(at[:, None] == slots[None, :], targets[None, :], 0), axis=1)
        ids = ids - shard_index * columns
        return head_stats(
            own,
            gain,
            at[:, None],
            ids[:, None],
            xs,
            (weight, left, right, far_low, far_high),
            dep,
            columns,
            offsets,
            targets.shape[0],
        )

    of_text = stats(text_slots, (text_all,), (early,))
    of_visual = stats(places, (rows, partner), ())
    both = (of_text + of_visual)[:3]

    def merged(pieces):
        tops, totals, chosen = pieces[:, 0], pieces[:, 1], pieces[:, 2]
        top = jnp.max(tops, axis=0)
        return jnp.stack(
            [top, jnp.sum(totals * jnp.exp(tops - top), axis=0), jnp.sum(chosen, axis=0)]
        )

    for turn in range(2):
        both = merged(jnp.stack([both, across(both, turn)]))
    both = both.reshape(3, sections, -1)
    both = lax.dynamic_index_in_dim(both, lax.axis_index("section"), 1, keepdims=False)
    top, total, chosen = merged(to_all(both, VOCAB))
    loss = top + jnp.log(total) - chosen
    return (pooled[None], loss[None])


def solution(mesh):
    in_specs = (
        P("dp", VOCAB, None, "section"),
        P(None, None, "section"),
        P("section"),
        P("section"),
        P("section"),
        P("section", VOCAB),
        P("dp", "section", VOCAB),
        P("dp", None),
        P(),
        P("dp", ("section",) + VOCAB),
        P("dp", None),
    )
    out_specs = (P("dp", VOCAB, "section"), P("dp", "section"))
    sizes = (mesh.shape["section"], mesh.shape["vocab"] // 8, 4, 2, mesh.shape["dp"])
    mesh = jax.sharding.Mesh(mesh.devices.reshape(sizes), ("section",) + VOCAB + ("dp",))
    return jax.shard_map(shards, mesh=mesh, in_specs=in_specs, out_specs=out_specs, check_vma=False)
```

```python
import functools

import jax
import jax.numpy as jnp
from jax import lax
from jax.experimental import pallas as pl
from jax.experimental.pallas import tpu as pltpu
from jax.sharding import PartitionSpec as P

WIDE = 256
VOCAB = ("zl", "y", "core")


def shifted(value, axis, step):
    count = lax.axis_size(axis)
    return lax.ppermute(value, axis, [((i + step) % count, i) for i in range(count)])


def extended(cells, axis, width):
    count = lax.axis_size(axis)
    ends = count - 1
    head, tail = cells[:width], cells[-width:]
    return jnp.concatenate(
        [
            lax.ppermute(tail, axis, [(i, (i + 1) % count) for i in range(ends)]),
            cells,
            lax.ppermute(head, axis, [((i + 1) % count, i) for i in range(ends)]),
        ],
        axis=0,
    )


def head_kernel(columns, offsets, from_text, own_ref, gain_ref, meta_ref, *refs):
    x_v, w_v, scaled, total, squares, sem_x, sem_w = refs[-7:]
    out_ref = refs[-8]
    w_low, w_own, w_left, w_right, w_far, w_off = refs[-14:-8]
    parts, lines, cores, rows, width = x_v.shape
    own, core = own_ref[0], own_ref[1]

    def block(j):
        return lax.rem(own + offsets[j], parts)

    def x_copies(j):
        if from_text:
            return [pltpu.make_async_copy(refs[0].at[block(j)], x_v.at[j], sem_x.at[j, 0])]
        return [
            pltpu.make_async_copy(
                refs[k].at[:, block(j)],
                x_v.at[j, :, core if k == 0 else 1 - core],
                sem_x.at[j, k],
            )
            for k in range(2)
        ]

    def w_copies(j):
        copies = [
            pltpu.make_async_copy(
                w_low.at[block(j)], w_v.at[j, pl.ds(0, WIDE)], sem_w.at[j, 0]
            )
        ]
        if j < 3:
            pieces = ((w_own, w_left, w_right)[j],)
        else:
            pieces = (w_far, w_off)
        size = WIDE // len(pieces)
        for k, piece in enumerate(pieces):
            copies.append(
                pltpu.make_async_copy(
                    piece, w_v.at[j, pl.ds(WIDE + k * size, size)], sem_w.at[j, k + 1]
                )
            )
        return copies

    for j in range(parts):
        for copy in x_copies(j) + w_copies(j):
            copy.start()
    for j in range(parts):
        for copy in x_copies(j):
            copy.wait()
        sums = jnp.zeros((rows, width), jnp.float32)
        for line in range(lines):
            for at in range(cores):
                piece = line * cores + at
                wide = x_v[j, line, at].astype(jnp.float32)
                sums = sums + wide * wide
                gain = gain_ref[block(j) * (lines * cores) + piece]
                scaled[:, piece * width : (piece + 1) * width] = (wide * gain).astype(
                    jnp.bfloat16
                )
        for copy in w_copies(j):
            copy.wait()
        part = lax.dot_general(
            scaled[...], w_v[j], (((1,), (1,)), ((), ())), preferred_element_type=jnp.float32
        )
        sums = jnp.sum(sums, axis=1, keepdims=True)
        if j == 0:
            total[...] = part
            squares[...] = sums
        else:
            total[...] += part
            squares[...] += sums
    factor = lax.rsqrt(squares[...] / (parts * lines * cores * width) + 1e-05)
    logits = total[...] * factor
    at = lax.broadcasted_iota(jnp.int32, logits.shape, 1)
    real = at < columns
    top = jnp.max(jnp.where(real, logits, -jnp.inf), axis=1, keepdims=True)
    summed = jnp.sum(
        jnp.where(real, jnp.exp(logits - top), 0.0), axis=1, keepdims=True
    )
    chosen = jnp.sum(
        jnp.where((at == meta_ref[:, 1:2]) & real, logits, 0.0), axis=1, keepdims=True
    )
    hit = (
        lax.broadcasted_iota(jnp.int32, (rows, out_ref.shape[1]), 1) == meta_ref[:, 0:1]
    )
    out_ref[...] = jnp.zeros(out_ref.shape, jnp.float32)
    for k, value in enumerate((top, summed, chosen)):
        out_ref[k : k + 1, :] = jnp.sum(jnp.where(hit, value, 0.0), axis=0, keepdims=True)


def head_stats(own, gain, meta, xs, weights, dep, columns, offsets, places):
    from_text = len(xs) == 1
    rows = meta.shape[0]
    parts, lines, cores = len(offsets), 4, 2
    width = xs[0].shape[-1]
    depth = lines * cores * width
    vmem = pl.BlockSpec(memory_space=pltpu.VMEM)
    anywhere = pl.BlockSpec(memory_space=pl.ANY)
    return pl.pallas_call(
        functools.partial(head_kernel, columns, offsets, from_text),
        out_shape=jax.ShapeDtypeStruct((8, places), jnp.float32),
        in_specs=[pl.BlockSpec(memory_space=pltpu.SMEM), vmem, vmem]
        + [anywhere] * (len(xs) + len(dep) + len(weights)),
        out_specs=vmem,
        scratch_shapes=[
            pltpu.VMEM((parts, lines, cores, rows, width), jnp.bfloat16),
            pltpu.VMEM((parts, 2 * WIDE, depth), jnp.bfloat16),
            pltpu.VMEM((rows, depth), jnp.bfloat16),
            pltpu.VMEM((rows, 2 * WIDE), jnp.float32),
            pltpu.VMEM((rows, 1), jnp.float32),
            pltpu.SemaphoreType.DMA((parts, 2)),
            pltpu.SemaphoreType.DMA((parts, 3)),
        ],
        compiler_params=pltpu.CompilerParams(vmem_limit_bytes=56 * 1024 * 1024),
        cost_estimate=pl.CostEstimate(
            flops=4 * rows * WIDE * parts * depth,
            bytes_accessed=2 * parts * depth * (rows + 2 * WIDE),
            transcendentals=2 * rows * WIDE,
        ),
    )(own, gain, meta, *xs, *dep, *weights)


def across(value, turn):
    count = lax.axis_size("section")
    pairs = [(i, i ^ 1) if turn == 0 else (i, count - 1 - i) for i in range(count)]
    return lax.ppermute(value, "section", pairs)


def to_all(value, axis):
    count = lax.axis_size(axis)
    return lax.all_to_all(jnp.broadcast_to(value[None], (count,) + value.shape), axis, 0, 0)


def shards(
    features,
    dw_weight,
    ln_gain,
    ln_bias,
    layer_scale,
    proj_weight,
    text_embed,
    positions,
    rms_gain,
    head_weight,
    labels,
):
    sections = lax.axis_size("section")
    parts = lax.axis_size("dp")
    shard_index = lax.axis_index(("section",) + VOCAB)
    places = positions[0]
    targets = labels[0]
    columns = head_weight.shape[1]
    slots = lax.iota(jnp.int32, targets.shape[0])

    text = to_all(text_embed[0], "section").reshape(slots.shape[0], -1)

    weight = head_weight.T
    low_all = lax.all_gather(weight[:WIDE], "dp", axis=0)
    high = jnp.pad(weight[WIDE:], ((0, 2 * WIDE - columns), (0, 0)))
    left, right = shifted(high, "dp", -1), shifted(high, "dp", 1)

    image = features[0]
    height, width, chans = image.shape
    padded = extended(image, VOCAB, 3)
    padded = jnp.pad(padded, ((0, 0), (3, 3), (0, 0))).astype(jnp.float32)
    conv = jnp.zeros((height, width, chans), jnp.float32)
    for row_off in range(7):
        for col_off in range(7):
            conv = (
                conv
                + padded[row_off : row_off + height, col_off : col_off + width]
                * dw_weight[row_off, col_off]
            )
    sums = jnp.stack(
        [jnp.sum(conv, axis=-1).reshape(-1), jnp.sum(conv * conv, axis=-1).reshape(-1)]
    )
    is_text = jnp.all(slots[:, None] != places[None, :], axis=1)
    rank = jnp.sum(
        jnp.where((slots[None, :] < slots[:, None]) & is_text[None, :], 1, 0), axis=1
    )
    text_rows = slots.shape[0] - places.shape[0]
    select = (rank[None, :] == lax.iota(jnp.int32, text_rows)[:, None]) & is_text[None, :]
    text, _ = lax.optimization_barrier((text, sums))
    text = jnp.dot(
        select.astype(jnp.bfloat16), text, preferred_element_type=jnp.float32
    ).astype(jnp.bfloat16)
    text_slots = jnp.sum(jnp.where(select, slots[None, :], 0), axis=1)
    text_all = lax.all_gather(text, VOCAB, axis=0)
    text_all = text_all.reshape(tuple(lax.axis_size(axis) for axis in VOCAB) + text.shape)
    sums = lax.psum(sums, "section")
    all_chans = chans * sections
    middle = sums[0].reshape(height, width) / all_chans
    spread = sums[1].reshape(height, width) / all_chans - middle * middle
    normal = (conv - middle[..., None]) * lax.rsqrt(spread + 1e-06)[..., None] * ln_gain + ln_bias
    block = image.astype(jnp.float32) + layer_scale * normal
    pooled = block.reshape(height // 4, 4, width // 4, 4, chans).mean(axis=(1, 3))
    pooled = pooled.reshape(-1, chans).astype(jnp.bfloat16)

    tokens = to_all(pooled, VOCAB).reshape(-1, chans)
    rows = jnp.dot(tokens, proj_weight, preferred_element_type=jnp.float32)
    for turn in range(2):
        rows = rows + across(rows.astype(jnp.bfloat16), turn).astype(jnp.float32)
    rows = rows.astype(jnp.bfloat16)

    rows, left, right = lax.optimization_barrier((rows, left, right))
    half = WIDE // 2
    far, off = shifted(left[:half], "dp", -1), shifted(right[half:], "dp", 1)
    rows = to_all(rows, "zl")
    rows, text_all, far, off = lax.optimization_barrier((rows, text_all, far, off))
    early = rows[0, :16, :128]
    rows = to_all(rows, "y")
    partner = lax.ppermute(rows, "core", [(0, 1), (1, 0)])

    gain = rms_gain.reshape(-1, 1, text.shape[1])
    own = jnp.stack([lax.axis_index("dp"), lax.axis_index("core")])
    offsets = (0, parts - 1, 1, 2)

    def stats(at, xs, dep):
        ids = jnp.sum(jnp.where(at[:, None] == slots[None, :], targets[None, :], 0), axis=1)
        ids = ids - shard_index * columns
        return head_stats(
            own,
            gain,
            jnp.stack([at, ids], axis=1),
            xs,
            (low_all, high, left, right, far, off),
            dep,
            columns,
            offsets,
            targets.shape[0],
        )

    of_text = stats(text_slots, (text_all,), (early,))
    of_visual = stats(places, (rows, partner), ())
    both = (of_text + of_visual)[:3]

    def merged(pieces):
        tops, totals, chosen = pieces[:, 0], pieces[:, 1], pieces[:, 2]
        top = jnp.max(tops, axis=0)
        return jnp.stack(
            [top, jnp.sum(totals * jnp.exp(tops - top), axis=0), jnp.sum(chosen, axis=0)]
        )

    for turn in range(2):
        both = merged(jnp.stack([both, across(both, turn)]))
    both = both.reshape(3, sections, -1)
    both = lax.dynamic_index_in_dim(both, lax.axis_index("section"), 1, keepdims=False)
    top, total, chosen = merged(to_all(both, VOCAB))
    loss = top + jnp.log(total) - chosen
    return (pooled[None], loss[None])


def solution(mesh):
    in_specs = (
        P("dp", VOCAB, None, "section"),
        P(None, None, "section"),
        P("section"),
        P("section"),
        P("section"),
        P("section", VOCAB),
        P("dp", "section", VOCAB),
        P("dp", None),
        P(),
        P("dp", ("section",) + VOCAB),
        P("dp", None),
    )
    out_specs = (P("dp", VOCAB, "section"), P("dp", "section"))
    sizes = (mesh.shape["section"], mesh.shape["vocab"] // 8, 4, 2, mesh.shape["dp"])
    mesh = jax.sharding.Mesh(mesh.devices.reshape(sizes), ("section",) + VOCAB + ("dp",))
    return jax.shard_map(shards, mesh=mesh, in_specs=in_specs, out_specs=out_specs, check_vma=False)
```

```python
import functools

import jax
import jax.numpy as jnp
from jax import lax
from jax.experimental import pallas as pl
from jax.experimental.pallas import tpu as pltpu
from jax.sharding import PartitionSpec as P

WIDE = 256
VOCAB = ("zl", "y", "core")


def shifted(value, axis, step):
    count = lax.axis_size(axis)
    return lax.ppermute(value, axis, [((i + step) % count, i) for i in range(count)])


def extended(cells, axis, width):
    count = lax.axis_size(axis)
    ends = count - 1
    head, tail = cells[:width], cells[-width:]
    above = lax.ppermute(tail, axis, [(i, (i + 1) % count) for i in range(ends)])
    below = lax.ppermute(head, axis, [((i + 1) % count, i) for i in range(ends)])
    return above, below


def head_kernel(columns, offsets, from_text, own_ref, gain_ref, meta_ref, *refs):
    x_v, w_v, scaled, total, squares, sem_x, sem_w = refs[-7:]
    out_ref = refs[-8]
    w_low, w_own, w_left, w_right, w_far, w_off = refs[-14:-8]
    parts, lines, cores, rows, width = x_v.shape
    own, core = own_ref[0], own_ref[1]

    def block(j):
        return lax.rem(own + offsets[j], parts)

    def x_copies(j):
        if from_text:
            return [pltpu.make_async_copy(refs[0].at[block(j)], x_v.at[j], sem_x.at[j, 0])]
        return [
            pltpu.make_async_copy(
                refs[k].at[:, block(j)],
                x_v.at[j, :, core if k == 0 else 1 - core],
                sem_x.at[j, k],
            )
            for k in range(2)
        ]

    def w_copies(j):
        copies = [
            pltpu.make_async_copy(
                w_low.at[block(j)], w_v.at[j, pl.ds(0, WIDE)], sem_w.at[j, 0]
            )
        ]
        if j < 3:
            pieces = ((w_own, w_left, w_right)[j],)
        else:
            pieces = (w_far, w_off)
        size = WIDE // len(pieces)
        for k, piece in enumerate(pieces):
            copies.append(
                pltpu.make_async_copy(
                    piece, w_v.at[j, pl.ds(WIDE + k * size, size)], sem_w.at[j, k + 1]
                )
            )
        return copies

    for j in range(parts):
        for copy in x_copies(j) + w_copies(j):
            copy.start()
    for j in range(parts):
        for copy in x_copies(j):
            copy.wait()
        sums = jnp.zeros((rows, width), jnp.float32)
        for line in range(lines):
            for at in range(cores):
                piece = line * cores + at
                wide = x_v[j, line, at].astype(jnp.float32)
                sums = sums + wide * wide
                gain = gain_ref[block(j) * (lines * cores) + piece]
                scaled[:, piece * width : (piece + 1) * width] = (wide * gain).astype(
                    jnp.bfloat16
                )
        for copy in w_copies(j):
            copy.wait()
        part = lax.dot_general(
            scaled[...], w_v[j], (((1,), (1,)), ((), ())), preferred_element_type=jnp.float32
        )
        sums = jnp.sum(sums, axis=1, keepdims=True)
        if j == 0:
            total[...] = part
            squares[...] = sums
        else:
            total[...] += part
            squares[...] += sums
    factor = lax.rsqrt(squares[...] / (parts * lines * cores * width) + 1e-05)
    logits = total[...] * factor
    at = lax.broadcasted_iota(jnp.int32, logits.shape, 1)
    real = at < columns
    top = jnp.max(jnp.where(real, logits, -jnp.inf), axis=1, keepdims=True)
    summed = jnp.sum(
        jnp.where(real, jnp.exp(logits - top), 0.0), axis=1, keepdims=True
    )
    chosen = jnp.sum(
        jnp.where((at == meta_ref[:, 1:2]) & real, logits, 0.0), axis=1, keepdims=True
    )
    hit = (
        lax.broadcasted_iota(jnp.int32, (rows, out_ref.shape[1]), 1) == meta_ref[:, 0:1]
    )
    out_ref[...] = jnp.zeros(out_ref.shape, jnp.float32)
    for k, value in enumerate((top, summed, chosen)):
        out_ref[k : k + 1, :] = jnp.sum(jnp.where(hit, value, 0.0), axis=0, keepdims=True)


def head_stats(own, gain, meta, xs, weights, dep, columns, offsets, places):
    from_text = len(xs) == 1
    rows = meta.shape[0]
    parts, lines, cores = len(offsets), 4, 2
    width = xs[0].shape[-1]
    depth = lines * cores * width
    vmem = pl.BlockSpec(memory_space=pltpu.VMEM)
    anywhere = pl.BlockSpec(memory_space=pl.ANY)
    return pl.pallas_call(
        functools.partial(head_kernel, columns, offsets, from_text),
        out_shape=jax.ShapeDtypeStruct((8, places), jnp.float32),
        in_specs=[pl.BlockSpec(memory_space=pltpu.SMEM), vmem, vmem]
        + [anywhere] * (len(xs) + len(dep) + len(weights)),
        out_specs=vmem,
        scratch_shapes=[
            pltpu.VMEM((parts, lines, cores, rows, width), jnp.bfloat16),
            pltpu.VMEM((parts, 2 * WIDE, depth), jnp.bfloat16),
            pltpu.VMEM((rows, depth), jnp.bfloat16),
            pltpu.VMEM((rows, 2 * WIDE), jnp.float32),
            pltpu.VMEM((rows, 1), jnp.float32),
            pltpu.SemaphoreType.DMA((parts, 2)),
            pltpu.SemaphoreType.DMA((parts, 3)),
        ],
        compiler_params=pltpu.CompilerParams(vmem_limit_bytes=56 * 1024 * 1024),
        cost_estimate=pl.CostEstimate(
            flops=4 * rows * WIDE * parts * depth,
            bytes_accessed=2 * parts * depth * (rows + 2 * WIDE),
            transcendentals=2 * rows * WIDE,
        ),
    )(own, gain, meta, *xs, *dep, *weights)


def across(value, turn):
    count = lax.axis_size("section")
    pairs = [(i, i ^ 1) if turn == 0 else (i, count - 1 - i) for i in range(count)]
    return lax.ppermute(value, "section", pairs)


def to_all(value, axis):
    count = lax.axis_size(axis)
    return lax.all_to_all(jnp.broadcast_to(value[None], (count,) + value.shape), axis, 0, 0)


def shards(
    features,
    dw_weight,
    ln_gain,
    ln_bias,
    layer_scale,
    proj_weight,
    text_embed,
    positions,
    rms_gain,
    head_weight,
    labels,
):
    sections = lax.axis_size("section")
    parts = lax.axis_size("dp")
    shard_index = lax.axis_index(("section",) + VOCAB)
    places = positions[0]
    targets = labels[0]
    columns = head_weight.shape[1]
    slots = lax.iota(jnp.int32, targets.shape[0])

    weight = head_weight.T
    low_all = lax.all_gather(weight[:WIDE], "dp", axis=0)
    high = jnp.pad(weight[WIDE:], ((0, 2 * WIDE - columns), (0, 0)))
    left, right = shifted(high, "dp", -1), shifted(high, "dp", 1)

    image = features[0]
    height, width, chans = image.shape
    above, below = extended(image, VOCAB, 3)
    padded = jnp.concatenate([above, image, below])

    text, _, _ = lax.optimization_barrier((text_embed[0], above, below))
    text = to_all(text, "section")

    padded = jnp.pad(padded, ((0, 0), (3, 3), (0, 0))).astype(jnp.float32)
    conv = jnp.zeros((height, width, chans), jnp.float32)
    for row_off in range(7):
        for col_off in range(7):
            conv = (
                conv
                + padded[row_off : row_off + height, col_off : col_off + width]
                * dw_weight[row_off, col_off]
            )
    sums = jnp.stack(
        [jnp.sum(conv, axis=-1).reshape(-1), jnp.sum(conv * conv, axis=-1).reshape(-1)]
    )
    sums = lax.psum(sums, "section")
    all_chans = chans * sections
    middle = sums[0].reshape(height, width) / all_chans
    spread = sums[1].reshape(height, width) / all_chans - middle * middle
    normal = (conv - middle[..., None]) * lax.rsqrt(spread + 1e-06)[..., None] * ln_gain + ln_bias
    block = image.astype(jnp.float32) + layer_scale * normal
    pooled = block.reshape(height // 4, 4, width // 4, 4, chans).mean(axis=(1, 3))
    pooled = pooled.reshape(-1, chans).astype(jnp.bfloat16)

    pooled, text = lax.optimization_barrier((pooled, text))
    tokens = to_all(pooled, VOCAB)
    rows = jnp.dot(tokens.reshape(-1, chans), proj_weight, preferred_element_type=jnp.float32)
    middle_row = rows.shape[0] // 2
    halves = [rows[:middle_row], rows[middle_row:]]
    for step in range(2):
        halves = [
            half + across(half.astype(jnp.bfloat16), step ^ at).astype(jnp.float32)
            for at, half in enumerate(halves)
        ]
    rows = jnp.concatenate([half.astype(jnp.bfloat16) for half in halves])

    is_text = jnp.all(slots[:, None] != places[None, :], axis=1)
    rank = jnp.sum(
        jnp.where((slots[None, :] < slots[:, None]) & is_text[None, :], 1, 0), axis=1
    )
    text_rows = slots.shape[0] - places.shape[0]
    select = (rank[None, :] == lax.iota(jnp.int32, text_rows)[:, None]) & is_text[None, :]
    text, _, _ = lax.optimization_barrier((text, tokens, low_all))
    text = jnp.dot(
        select.astype(jnp.bfloat16),
        text.reshape(slots.shape[0], -1),
        preferred_element_type=jnp.float32,
    ).astype(jnp.bfloat16)
    text_slots = jnp.sum(jnp.where(select, slots[None, :], 0), axis=1)
    text_all = lax.all_gather(text, VOCAB, axis=0)
    text_all = text_all.reshape(tuple(lax.axis_size(axis) for axis in VOCAB) + text.shape)

    rows, left, right = lax.optimization_barrier((rows, left, right))
    half = WIDE // 2
    far, off = shifted(left[:half], "dp", -1), shifted(right[half:], "dp", 1)
    rows = to_all(rows, "zl")
    early = rows
    rows = to_all(rows, "y")
    rows, text_all, far, off = lax.optimization_barrier((rows, text_all, far, off))
    partner = lax.ppermute(rows, "core", [(0, 1), (1, 0)])

    gain = rms_gain.reshape(-1, 1, text.shape[1])
    own = jnp.stack([lax.axis_index("dp"), lax.axis_index("core")])
    offsets = (0, parts - 1, 1, 2)

    def stats(at, xs, dep):
        ids = jnp.sum(jnp.where(at[:, None] == slots[None, :], targets[None, :], 0), axis=1)
        ids = ids - shard_index * columns
        return head_stats(
            own,
            gain,
            jnp.stack([at, ids], axis=1),
            xs,
            (low_all, high, left, right, far, off),
            dep,
            columns,
            offsets,
            targets.shape[0],
        )

    of_text = stats(text_slots, (text_all,), (early,))
    of_visual = stats(places, (rows, partner), ())
    both = (of_text + of_visual)[:3]

    def merged(pieces):
        tops, totals, chosen = pieces[:, 0], pieces[:, 1], pieces[:, 2]
        top = jnp.max(tops, axis=0)
        return jnp.stack(
            [top, jnp.sum(totals * jnp.exp(tops - top), axis=0), jnp.sum(chosen, axis=0)]
        )

    section = lax.axis_index("section")
    mine = lax.iota(jnp.int32, sections)[:, None, None] == section
    both = lax.psum(jnp.where(mine, both[None], 0.0), "section")
    both = both.reshape(sections, 3, sections, -1)
    both = merged(lax.dynamic_index_in_dim(both, section, 2, keepdims=False))
    top, total, chosen = merged(to_all(both, VOCAB))
    loss = top + jnp.log(total) - chosen
    return (pooled[None], loss[None])


def solution(mesh):
    in_specs = (
        P("dp", VOCAB, None, "section"),
        P(None, None, "section"),
        P("section"),
        P("section"),
        P("section"),
        P("section", VOCAB),
        P("dp", "section", VOCAB),
        P("dp", None),
        P(),
        P("dp", ("section",) + VOCAB),
        P("dp", None),
    )
    out_specs = (P("dp", VOCAB, "section"), P("dp", "section"))
    sizes = (mesh.shape["section"], mesh.shape["vocab"] // 8, 4, 2, mesh.shape["dp"])
    mesh = jax.sharding.Mesh(mesh.devices.reshape(sizes), ("section",) + VOCAB + ("dp",))
    return jax.shard_map(shards, mesh=mesh, in_specs=in_specs, out_specs=out_specs, check_vma=False)
```

```python
import functools

import jax
import jax.numpy as jnp
from jax import lax
from jax.experimental import pallas as pl
from jax.experimental.pallas import tpu as pltpu
from jax.sharding import PartitionSpec as P

WIDE = 256
VOCAB = ("zl", "y", "core")


def shifted(value, axis, step):
    count = lax.axis_size(axis)
    return lax.ppermute(value, axis, [((i + step) % count, i) for i in range(count)])


def extended(cells, axis, width):
    count = lax.axis_size(axis)
    ends = count - 1
    head, tail = cells[:width], cells[-width:]
    above = lax.ppermute(tail, axis, [(i, (i + 1) % count) for i in range(ends)])
    below = lax.ppermute(head, axis, [((i + 1) % count, i) for i in range(ends)])
    return above, below


def head_kernel(columns, offsets, from_text, own_ref, gain_ref, meta_ref, *refs):
    x_v, w_v, scaled, total, squares, sem_x, sem_w = refs[-7:]
    out_ref = refs[-8]
    w_low, w_own, w_left, w_right, w_far, w_off = refs[-14:-8]
    parts, lines, cores, rows, width = x_v.shape
    own, core = own_ref[0], own_ref[1]

    def block(j):
        return lax.rem(own + offsets[j], parts)

    def x_copies(j):
        return [
            pltpu.make_async_copy(
                refs[k].at[block(j)] if from_text else refs[k].at[:, block(j)],
                x_v.at[j, :, core if k == 0 else 1 - core],
                sem_x.at[j, k],
            )
            for k in range(2)
        ]

    def w_copies(j):
        copies = [
            pltpu.make_async_copy(
                w_low.at[block(j)], w_v.at[j, pl.ds(0, WIDE)], sem_w.at[j, 0]
            )
        ]
        if j < 3:
            pieces = ((w_own, w_left, w_right)[j],)
        else:
            pieces = (w_far, w_off)
        size = WIDE // len(pieces)
        for k, piece in enumerate(pieces):
            copies.append(
                pltpu.make_async_copy(
                    piece, w_v.at[j, pl.ds(WIDE + k * size, size)], sem_w.at[j, k + 1]
                )
            )
        return copies

    for j in range(parts):
        for copy in x_copies(j) + w_copies(j):
            copy.start()
    def scale(j):
        for copy in x_copies(j):
            copy.wait()
        sums = jnp.zeros((rows, width), jnp.float32)
        for line in range(lines):
            for at in range(cores):
                piece = line * cores + at
                wide = x_v[j, line, at].astype(jnp.float32)
                sums = sums + wide * wide
                gain = gain_ref[block(j) * (lines * cores) + piece]
                scaled[j % 2, :, piece * width : (piece + 1) * width] = (
                    wide * gain
                ).astype(jnp.bfloat16)
        sums = jnp.sum(sums, axis=1, keepdims=True)
        if j == 0:
            squares[...] = sums
        else:
            squares[...] += sums

    scale(0)
    for j in range(parts):
        for copy in w_copies(j):
            copy.wait()
        if j + 1 < parts:
            scale(j + 1)
        part = lax.dot_general(
            scaled[j % 2],
            w_v[j],
            (((1,), (1,)), ((), ())),
            preferred_element_type=jnp.float32,
        )
        if j == 0:
            total[...] = part
        else:
            total[...] += part
    factor = lax.rsqrt(squares[...] / (parts * lines * cores * width) + 1e-05)
    logits = total[...] * factor
    at = lax.broadcasted_iota(jnp.int32, logits.shape, 1)
    real = at < columns
    top = jnp.max(jnp.where(real, logits, -jnp.inf), axis=1, keepdims=True)
    summed = jnp.sum(
        jnp.where(real, jnp.exp(logits - top), 0.0), axis=1, keepdims=True
    )
    chosen = jnp.sum(
        jnp.where((at == meta_ref[:, 1:2]) & real, logits, 0.0), axis=1, keepdims=True
    )
    hit = (
        lax.broadcasted_iota(jnp.int32, (rows, out_ref.shape[1]), 1) == meta_ref[:, 0:1]
    )
    out_ref[...] = jnp.zeros(out_ref.shape, jnp.float32)
    for k, value in enumerate((top, summed, chosen)):
        out_ref[k : k + 1, :] = jnp.sum(jnp.where(hit, value, 0.0), axis=0, keepdims=True)


def head_stats(own, gain, meta, xs, weights, dep, columns, offsets, places):
    from_text = len(dep) == 1
    rows = meta.shape[0]
    parts, lines, cores = len(offsets), 4, 2
    width = xs[0].shape[-1]
    depth = lines * cores * width
    vmem = pl.BlockSpec(memory_space=pltpu.VMEM)
    anywhere = pl.BlockSpec(memory_space=pl.ANY)
    return pl.pallas_call(
        functools.partial(head_kernel, columns, offsets, from_text),
        out_shape=jax.ShapeDtypeStruct((8, places), jnp.float32),
        in_specs=[pl.BlockSpec(memory_space=pltpu.SMEM), vmem, vmem]
        + [anywhere] * (len(xs) + len(dep) + len(weights)),
        out_specs=vmem,
        scratch_shapes=[
            pltpu.VMEM((parts, lines, cores, rows, width), jnp.bfloat16),
            pltpu.VMEM((parts, 2 * WIDE, depth), jnp.bfloat16),
            pltpu.VMEM((2, rows, depth), jnp.bfloat16),
            pltpu.VMEM((rows, 2 * WIDE), jnp.float32),
            pltpu.VMEM((rows, 1), jnp.float32),
            pltpu.SemaphoreType.DMA((parts, 2)),
            pltpu.SemaphoreType.DMA((parts, 3)),
        ],
        compiler_params=pltpu.CompilerParams(vmem_limit_bytes=56 * 1024 * 1024),
        cost_estimate=pl.CostEstimate(
            flops=4 * rows * WIDE * parts * depth,
            bytes_accessed=2 * parts * depth * (rows + 2 * WIDE),
            transcendentals=2 * rows * WIDE,
        ),
    )(own, gain, meta, *xs, *dep, *weights)


def across(value, turn):
    count = lax.axis_size("section")
    pairs = [(i, i ^ 1) if turn == 0 else (i, count - 1 - i) for i in range(count)]
    return lax.ppermute(value, "section", pairs)


def to_all(value, axis):
    count = lax.axis_size(axis)
    return lax.all_to_all(jnp.broadcast_to(value[None], (count,) + value.shape), axis, 0, 0)


def shards(
    features,
    dw_weight,
    ln_gain,
    ln_bias,
    layer_scale,
    proj_weight,
    text_embed,
    positions,
    rms_gain,
    head_weight,
    labels,
):
    sections = lax.axis_size("section")
    parts = lax.axis_size("dp")
    shard_index = lax.axis_index(("section",) + VOCAB)
    places = positions[0]
    targets = labels[0]
    columns = head_weight.shape[1]
    slots = lax.iota(jnp.int32, targets.shape[0])

    weight = head_weight.T
    low_all = lax.all_gather(weight[:WIDE], "dp", axis=0)
    high = jnp.pad(weight[WIDE:], ((0, 2 * WIDE - columns), (0, 0)))
    left, right = shifted(high, "dp", -1), shifted(high, "dp", 1)

    text_all = lax.all_gather(text_embed[0], ("section", "zl", "y"), axis=0)
    is_text = jnp.all(slots[:, None] != places[None, :], axis=1)
    rank = jnp.sum(
        jnp.where((slots[None, :] < slots[:, None]) & is_text[None, :], 1, 0), axis=1
    )
    text_rows = slots.shape[0] - places.shape[0]
    select = (rank[None, :] == lax.iota(jnp.int32, text_rows)[:, None]) & is_text[None, :]
    text_slots = jnp.sum(jnp.where(select, slots[None, :], 0), axis=1)
    text = jnp.einsum(
        "jsr,szyrc->zyjc",
        select.astype(jnp.bfloat16).reshape(text_rows, sections, -1),
        text_all.reshape(
            (sections, lax.axis_size("zl"), lax.axis_size("y")) + text_all.shape[1:]
        ),
        preferred_element_type=jnp.float32,
    ).astype(jnp.bfloat16)
    text_partner = lax.ppermute(text, "core", [(0, 1), (1, 0)])

    image = features[0]
    height, width, chans = image.shape
    above, below = extended(image, VOCAB, 3)
    padded = jnp.concatenate([above, image, below])

    padded = jnp.pad(padded, ((0, 0), (3, 3), (0, 0))).astype(jnp.float32)
    conv = jnp.zeros((height, width, chans), jnp.float32)
    for row_off in range(7):
        for col_off in range(7):
            conv = (
                conv
                + padded[row_off : row_off + height, col_off : col_off + width]
                * dw_weight[row_off, col_off]
            )
    sums = jnp.stack(
        [jnp.sum(conv, axis=-1).reshape(-1), jnp.sum(conv * conv, axis=-1).reshape(-1)]
    )
    sums = lax.psum(sums, "section")
    all_chans = chans * sections
    middle = sums[0].reshape(height, width) / all_chans
    spread = sums[1].reshape(height, width) / all_chans - middle * middle
    normal = (conv - middle[..., None]) * lax.rsqrt(spread + 1e-06)[..., None] * ln_gain + ln_bias
    block = image.astype(jnp.float32) + layer_scale * normal
    pooled = block.reshape(height // 4, 4, width // 4, 4, chans).mean(axis=(1, 3))
    pooled = pooled.reshape(-1, chans).astype(jnp.bfloat16)

    tokens = to_all(pooled, VOCAB)
    rows = jnp.dot(tokens.reshape(-1, chans), proj_weight, preferred_element_type=jnp.float32)
    middle_row = rows.shape[0] // 2
    halves = [rows[:middle_row], rows[middle_row:]]
    for step in range(2):
        halves = [
            half + across(half.astype(jnp.bfloat16), step ^ at).astype(jnp.float32)
            for at, half in enumerate(halves)
        ]
    rows = jnp.concatenate([half.astype(jnp.bfloat16) for half in halves])

    rows, left, right = lax.optimization_barrier((rows, left, right))
    half = WIDE // 2
    far, off = shifted(left[:half], "dp", -1), shifted(right[half:], "dp", 1)
    rows = to_all(rows, "zl")
    early = rows
    rows = to_all(rows, "y")
    rows, text, far, off, low_all = lax.optimization_barrier((rows, text, far, off, low_all))
    partner = lax.ppermute(rows, "core", [(0, 1), (1, 0)])

    gain = rms_gain.reshape(-1, 1, text_embed.shape[2])
    own = jnp.stack([lax.axis_index("dp"), lax.axis_index("core")])
    offsets = (0, parts - 1, 1, 2)

    def stats(at, xs, dep):
        ids = jnp.sum(jnp.where(at[:, None] == slots[None, :], targets[None, :], 0), axis=1)
        ids = ids - shard_index * columns
        return head_stats(
            own,
            gain,
            jnp.stack([at, ids], axis=1),
            xs,
            (low_all, high, left, right, far, off),
            dep,
            columns,
            offsets,
            targets.shape[0],
        )

    of_text = stats(text_slots, (text, text_partner), (early,))
    of_visual = stats(places, (rows, partner), ())
    both = (of_text + of_visual)[:3]

    def merged(pieces):
        tops, totals, chosen = pieces[:, 0], pieces[:, 1], pieces[:, 2]
        top = jnp.max(tops, axis=0)
        return jnp.stack(
            [top, jnp.sum(totals * jnp.exp(tops - top), axis=0), jnp.sum(chosen, axis=0)]
        )

    section = lax.axis_index("section")
    mine = lax.iota(jnp.int32, sections)[:, None, None] == section
    both = lax.psum(jnp.where(mine, both[None], 0.0), "section")
    both = both.reshape(sections, 3, sections, -1)
    both = merged(lax.dynamic_index_in_dim(both, section, 2, keepdims=False))
    top, total, chosen = merged(to_all(both, VOCAB))
    loss = top + jnp.log(total) - chosen
    return (pooled[None], loss[None])


def solution(mesh):
    in_specs = (
        P("dp", VOCAB, None, "section"),
        P(None, None, "section"),
        P("section"),
        P("section"),
        P("section"),
        P("section", VOCAB),
        P("dp", "section", VOCAB),
        P("dp", None),
        P(),
        P("dp", ("section",) + VOCAB),
        P("dp", None),
    )
    out_specs = (P("dp", VOCAB, "section"), P("dp", "section"))
    sizes = (mesh.shape["section"], mesh.shape["vocab"] // 8, 4, 2, mesh.shape["dp"])
    mesh = jax.sharding.Mesh(mesh.devices.reshape(sizes), ("section",) + VOCAB + ("dp",))
    return jax.shard_map(shards, mesh=mesh, in_specs=in_specs, out_specs=out_specs, check_vma=False)
```

```python
import functools

import jax
import jax.numpy as jnp
from jax import lax
from jax.experimental import pallas as pl
from jax.experimental.pallas import tpu as pltpu
from jax.sharding import PartitionSpec as P

WIDE = 256
LOW = 192
VOCAB = ("zl", "y", "core")


def shifted(value, axis, step):
    count = lax.axis_size(axis)
    return lax.ppermute(value, axis, [((i + step) % count, i) for i in range(count)])


def extended(cells, axis, width):
    count = lax.axis_size(axis)
    ends = count - 1
    head, tail = cells[:width], cells[-width:]
    above = lax.ppermute(tail, axis, [(i, (i + 1) % count) for i in range(ends)])
    below = lax.ppermute(head, axis, [((i + 1) % count, i) for i in range(ends)])
    return above, below


def head_kernel(columns, offsets, from_text, own_ref, gain_ref, meta_ref, *refs):
    x_v, w_v, scaled, total, squares, sem_x, sem_w = refs[-7:]
    out_ref = refs[-8]
    w_low, w_own, w_left, w_right, w_far, w_off = refs[-14:-8]
    parts, lines, cores, rows, width = x_v.shape
    own, core = own_ref[0], own_ref[1]

    def block(j):
        return lax.rem(own + offsets[j], parts)

    def x_copies(j):
        if from_text:
            return [
                pltpu.make_async_copy(refs[0].at[:, :, block(j)], x_v.at[j], sem_x.at[j, 0])
            ]
        return [
            pltpu.make_async_copy(
                refs[k].at[:, block(j)],
                x_v.at[j, :, core if k == 0 else 1 - core],
                sem_x.at[j, k],
            )
            for k in range(2)
        ]

    def w_copies(j):
        copies = [
            pltpu.make_async_copy(
                w_low.at[block(j)], w_v.at[j, pl.ds(0, LOW)], sem_w.at[j, 0]
            )
        ]
        if j < 3:
            pieces = ((w_own, w_left, w_right)[j],)
        else:
            pieces = (w_far, w_off)
        size = (2 * WIDE - LOW) // len(pieces)
        for k, piece in enumerate(pieces):
            copies.append(
                pltpu.make_async_copy(
                    piece, w_v.at[j, pl.ds(LOW + k * size, size)], sem_w.at[j, k + 1]
                )
            )
        return copies

    for j in range(parts):
        for copy in x_copies(j) + w_copies(j):
            copy.start()
    def scale(j):
        for copy in x_copies(j):
            copy.wait()
        sums = jnp.zeros((rows, width), jnp.float32)
        for line in range(lines):
            for at in range(cores):
                piece = line * cores + at
                wide = x_v[j, line, at].astype(jnp.float32)
                sums = sums + wide * wide
                gain = gain_ref[block(j) * (lines * cores) + piece]
                scaled[j % 2, :, piece * width : (piece + 1) * width] = (
                    wide * gain
                ).astype(jnp.bfloat16)
        sums = jnp.sum(sums, axis=1, keepdims=True)
        if j == 0:
            squares[...] = sums
        else:
            squares[...] += sums

    scale(0)
    for j in range(parts):
        for copy in w_copies(j):
            copy.wait()
        if j + 1 < parts:
            scale(j + 1)
        part = lax.dot_general(
            scaled[j % 2],
            w_v[j],
            (((1,), (1,)), ((), ())),
            preferred_element_type=jnp.float32,
        )
        if j == 0:
            total[...] = part
        else:
            total[...] += part
    factor = lax.rsqrt(squares[...] / (parts * lines * cores * width) + 1e-05)
    logits = total[...] * factor
    at = lax.broadcasted_iota(jnp.int32, logits.shape, 1)
    real = at < columns
    top = jnp.max(jnp.where(real, logits, -jnp.inf), axis=1, keepdims=True)
    summed = jnp.sum(
        jnp.where(real, jnp.exp(logits - top), 0.0), axis=1, keepdims=True
    )
    chosen = jnp.sum(
        jnp.where((at == meta_ref[:, 1:2]) & real, logits, 0.0), axis=1, keepdims=True
    )
    hit = (
        lax.broadcasted_iota(jnp.int32, (rows, out_ref.shape[1]), 1) == meta_ref[:, 0:1]
    )
    out_ref[...] = jnp.zeros(out_ref.shape, jnp.float32)
    for k, value in enumerate((top, summed, chosen)):
        out_ref[k : k + 1, :] = jnp.sum(jnp.where(hit, value, 0.0), axis=0, keepdims=True)


def head_stats(own, gain, meta, xs, weights, dep, columns, offsets, places):
    from_text = len(dep) == 1
    rows = meta.shape[0]
    parts, lines, cores = len(offsets), 4, 2
    width = xs[0].shape[-1]
    depth = lines * cores * width
    vmem = pl.BlockSpec(memory_space=pltpu.VMEM)
    anywhere = pl.BlockSpec(memory_space=pl.ANY)
    return pl.pallas_call(
        functools.partial(head_kernel, columns, offsets, from_text),
        out_shape=jax.ShapeDtypeStruct((8, places), jnp.float32),
        in_specs=[pl.BlockSpec(memory_space=pltpu.SMEM), vmem, vmem]
        + [anywhere] * (len(xs) + len(dep) + len(weights)),
        out_specs=vmem,
        scratch_shapes=[
            pltpu.VMEM((parts, lines, cores, rows, width), jnp.bfloat16),
            pltpu.VMEM((parts, 2 * WIDE, depth), jnp.bfloat16),
            pltpu.VMEM((2, rows, depth), jnp.bfloat16),
            pltpu.VMEM((rows, 2 * WIDE), jnp.float32),
            pltpu.VMEM((rows, 1), jnp.float32),
            pltpu.SemaphoreType.DMA((parts, 2)),
            pltpu.SemaphoreType.DMA((parts, 3)),
        ],
        compiler_params=pltpu.CompilerParams(vmem_limit_bytes=56 * 1024 * 1024),
        cost_estimate=pl.CostEstimate(
            flops=4 * rows * WIDE * parts * depth,
            bytes_accessed=2 * parts * depth * (rows + 2 * WIDE),
            transcendentals=2 * rows * WIDE,
        ),
    )(own, gain, meta, *xs, *dep, *weights)


def across(value, turn):
    count = lax.axis_size("section")
    pairs = [(i, i ^ 1) if turn == 0 else (i, count - 1 - i) for i in range(count)]
    return lax.ppermute(value, "section", pairs)


def to_all(value, axis):
    count = lax.axis_size(axis)
    return lax.all_to_all(jnp.broadcast_to(value[None], (count,) + value.shape), axis, 0, 0)


def shards(
    features,
    dw_weight,
    ln_gain,
    ln_bias,
    layer_scale,
    proj_weight,
    text_embed,
    positions,
    rms_gain,
    head_weight,
    labels,
):
    sections = lax.axis_size("section")
    parts = lax.axis_size("dp")
    shard_index = lax.axis_index(("section",) + VOCAB)
    places = positions[0]
    targets = labels[0]
    columns = head_weight.shape[1]
    slots = lax.iota(jnp.int32, targets.shape[0])

    weight = head_weight.T
    low_all = lax.all_gather(weight[:LOW], "dp", axis=0)
    high = jnp.pad(weight[LOW:], ((0, 2 * WIDE - columns), (0, 0)))
    left, right = shifted(high, "dp", -1), shifted(high, "dp", 1)

    text = lax.all_gather(text_embed[0], ("section", "zl"), axis=0)
    is_text = jnp.all(slots[:, None] != places[None, :], axis=1)
    rank = jnp.sum(
        jnp.where((slots[None, :] < slots[:, None]) & is_text[None, :], 1, 0), axis=1
    )
    text_rows = slots.shape[0] - places.shape[0]
    select = (rank[None, :] == lax.iota(jnp.int32, text_rows)[:, None]) & is_text[None, :]
    text_slots = jnp.sum(jnp.where(select, slots[None, :], 0), axis=1)
    image = features[0]
    height, width, chans = image.shape
    above, below = extended(image, VOCAB, 3)
    padded = jnp.concatenate([above, image, below])

    padded = jnp.pad(padded, ((0, 0), (3, 3), (0, 0))).astype(jnp.float32)
    conv = jnp.zeros((height, width, chans), jnp.float32)
    for row_off in range(7):
        for col_off in range(7):
            conv = (
                conv
                + padded[row_off : row_off + height, col_off : col_off + width]
                * dw_weight[row_off, col_off]
            )
    sums = jnp.stack(
        [jnp.sum(conv, axis=-1).reshape(-1), jnp.sum(conv * conv, axis=-1).reshape(-1)]
    )
    sums = lax.psum(sums, "section")
    all_chans = chans * sections
    middle = sums[0].reshape(height, width) / all_chans
    spread = sums[1].reshape(height, width) / all_chans - middle * middle
    normal = (conv - middle[..., None]) * lax.rsqrt(spread + 1e-06)[..., None] * ln_gain + ln_bias
    block = image.astype(jnp.float32) + layer_scale * normal
    pooled = block.reshape(height // 4, 4, width // 4, 4, chans).mean(axis=(1, 3))
    pooled = pooled.reshape(-1, chans).astype(jnp.bfloat16)

    tokens = to_all(pooled, VOCAB)
    text, _ = lax.optimization_barrier((text, tokens))
    text = jnp.einsum(
        "jsr,szrc->zjc",
        select.astype(jnp.bfloat16).reshape(text_rows, sections, -1),
        text.reshape((sections, -1) + text.shape[1:]),
        preferred_element_type=jnp.float32,
    ).astype(jnp.bfloat16)
    text_all = lax.all_gather(text, ("y", "core"), axis=0)
    text_all = text_all.reshape((lax.axis_size("y"), lax.axis_size("core")) + text.shape)
    rows = jnp.dot(tokens.reshape(-1, chans), proj_weight, preferred_element_type=jnp.float32)
    middle_row = rows.shape[0] // 2
    halves = [rows[:middle_row], rows[middle_row:]]
    for step in range(2):
        halves = [
            half + across(half.astype(jnp.bfloat16), step ^ at).astype(jnp.float32)
            for at, half in enumerate(halves)
        ]
    rows = jnp.concatenate([half.astype(jnp.bfloat16) for half in halves])

    rows, left, right = lax.optimization_barrier((rows, left, right))
    half = high.shape[0] // 2
    far, off = shifted(left[:half], "dp", -1), shifted(right[half:], "dp", 1)
    rows = to_all(rows, "zl")
    early = rows
    rows = to_all(rows, "y")
    rows, text_all, far, off = lax.optimization_barrier((rows, text_all, far, off))
    partner = lax.ppermute(rows, "core", [(0, 1), (1, 0)])

    gain = rms_gain.reshape(-1, 1, text_embed.shape[2])
    own = jnp.stack([lax.axis_index("dp"), lax.axis_index("core")])
    offsets = (0, parts - 1, 1, 2)

    def stats(at, xs, dep):
        ids = jnp.sum(jnp.where(at[:, None] == slots[None, :], targets[None, :], 0), axis=1)
        ids = ids - shard_index * columns
        return head_stats(
            own,
            gain,
            jnp.stack([at, ids], axis=1),
            xs,
            (low_all, high, left, right, far, off),
            dep,
            columns,
            offsets,
            targets.shape[0],
        )

    of_text = stats(text_slots, (text_all,), (early,))
    of_visual = stats(places, (rows, partner), ())
    both = (of_text + of_visual)[:3]

    def merged(pieces):
        tops, totals, chosen = pieces[:, 0], pieces[:, 1], pieces[:, 2]
        top = jnp.max(tops, axis=0)
        return jnp.stack(
            [top, jnp.sum(totals * jnp.exp(tops - top), axis=0), jnp.sum(chosen, axis=0)]
        )

    section = lax.axis_index("section")
    mine = lax.iota(jnp.int32, sections)[:, None, None] == section
    both = lax.psum(jnp.where(mine, both[None], 0.0), "section")
    both = both.reshape(sections, 3, sections, -1)
    both = merged(lax.dynamic_index_in_dim(both, section, 2, keepdims=False))
    top, total, chosen = merged(to_all(both, VOCAB))
    loss = top + jnp.log(total) - chosen
    return (pooled[None], loss[None])


def solution(mesh):
    in_specs = (
        P("dp", VOCAB, None, "section"),
        P(None, None, "section"),
        P("section"),
        P("section"),
        P("section"),
        P("section", VOCAB),
        P("dp", "section", VOCAB),
        P("dp", None),
        P(),
        P("dp", ("section",) + VOCAB),
        P("dp", None),
    )
    out_specs = (P("dp", VOCAB, "section"), P("dp", "section"))
    sizes = (mesh.shape["section"], mesh.shape["vocab"] // 8, 4, 2, mesh.shape["dp"])
    mesh = jax.sharding.Mesh(mesh.devices.reshape(sizes), ("section",) + VOCAB + ("dp",))
    return jax.shard_map(shards, mesh=mesh, in_specs=in_specs, out_specs=out_specs, check_vma=False)
```

```python
import functools

import jax
import jax.numpy as jnp
from jax import lax
from jax.experimental import pallas as pl
from jax.experimental.pallas import tpu as pltpu
from jax.sharding import PartitionSpec as P

WIDE = 256
LOW = 64
VOCAB = ("zl", "y", "core")


def shifted(value, axis, step):
    count = lax.axis_size(axis)
    return lax.ppermute(value, axis, [((i + step) % count, i) for i in range(count)])


def extended(cells, axis, width):
    count = lax.axis_size(axis)
    ends = count - 1
    head, tail = cells[:width], cells[-width:]
    above = lax.ppermute(tail, axis, [(i, (i + 1) % count) for i in range(ends)])
    below = lax.ppermute(head, axis, [((i + 1) % count, i) for i in range(ends)])
    return above, below


def head_kernel(columns, offsets, from_text, own_ref, gain_ref, meta_ref, *refs):
    x_v, w_v, scaled, total, squares, sem_x, sem_w = refs[-7:]
    out_ref = refs[-8]
    w_low, w_own, w_left, w_right, w_far, w_off = refs[-14:-8]
    parts, lines, cores, rows, width = x_v.shape
    own, core = own_ref[0], own_ref[1]

    def block(j):
        return lax.rem(own + offsets[j], parts)

    def x_copies(j):
        if from_text:
            return [
                pltpu.make_async_copy(refs[0].at[:, :, block(j)], x_v.at[j], sem_x.at[j, 0])
            ]
        return [
            pltpu.make_async_copy(
                refs[k].at[:, block(j)],
                x_v.at[j, :, core if k == 0 else 1 - core],
                sem_x.at[j, k],
            )
            for k in range(2)
        ]

    def w_copies(j):
        copies = [
            pltpu.make_async_copy(
                w_low.at[block(j)], w_v.at[j, pl.ds(0, LOW)], sem_w.at[j, 0]
            )
        ]
        if j < 3:
            pieces = ((w_own, w_left, w_right)[j],)
        else:
            pieces = (w_far, w_off)
        size = (2 * WIDE - LOW) // len(pieces)
        for k, piece in enumerate(pieces):
            copies.append(
                pltpu.make_async_copy(
                    piece, w_v.at[j, pl.ds(LOW + k * size, size)], sem_w.at[j, k + 1]
                )
            )
        return copies

    for j in range(parts):
        for copy in x_copies(j) + w_copies(j):
            copy.start()
    def scale(j):
        for copy in x_copies(j):
            copy.wait()
        sums = jnp.zeros((rows, width), jnp.float32)
        for line in range(lines):
            for at in range(cores):
                piece = line * cores + at
                wide = x_v[j, line, at].astype(jnp.float32)
                sums = sums + wide * wide
                gain = gain_ref[block(j) * (lines * cores) + piece]
                scaled[j % 2, :, piece * width : (piece + 1) * width] = (
                    wide * gain
                ).astype(jnp.bfloat16)
        sums = jnp.sum(sums, axis=1, keepdims=True)
        if j == 0:
            squares[...] = sums
        else:
            squares[...] += sums

    scale(0)
    for j in range(parts):
        for copy in w_copies(j):
            copy.wait()
        if j + 1 < parts:
            scale(j + 1)
        part = lax.dot_general(
            scaled[j % 2],
            w_v[j],
            (((1,), (1,)), ((), ())),
            preferred_element_type=jnp.float32,
        )
        if j == 0:
            total[...] = part
        else:
            total[...] += part
    factor = lax.rsqrt(squares[...] / (parts * lines * cores * width) + 1e-05)
    logits = total[...] * factor
    at = lax.broadcasted_iota(jnp.int32, logits.shape, 1)
    real = at < columns
    top = jnp.max(jnp.where(real, logits, -jnp.inf), axis=1, keepdims=True)
    summed = jnp.sum(
        jnp.where(real, jnp.exp(logits - top), 0.0), axis=1, keepdims=True
    )
    chosen = jnp.sum(
        jnp.where((at == meta_ref[:, 1:2]) & real, logits, 0.0), axis=1, keepdims=True
    )
    hit = (
        lax.broadcasted_iota(jnp.int32, (rows, out_ref.shape[1]), 1) == meta_ref[:, 0:1]
    )
    out_ref[...] = jnp.zeros(out_ref.shape, jnp.float32)
    for k, value in enumerate((top, summed, chosen)):
        out_ref[k : k + 1, :] = jnp.sum(jnp.where(hit, value, 0.0), axis=0, keepdims=True)


def head_stats(own, gain, meta, xs, weights, dep, columns, offsets, places):
    from_text = len(dep) == 1
    rows = meta.shape[0]
    parts, lines, cores = len(offsets), 4, 2
    width = xs[0].shape[-1]
    depth = lines * cores * width
    vmem = pl.BlockSpec(memory_space=pltpu.VMEM)
    anywhere = pl.BlockSpec(memory_space=pl.ANY)
    return pl.pallas_call(
        functools.partial(head_kernel, columns, offsets, from_text),
        out_shape=jax.ShapeDtypeStruct((8, places), jnp.float32),
        in_specs=[pl.BlockSpec(memory_space=pltpu.SMEM), vmem, vmem]
        + [anywhere] * (len(xs) + len(dep) + len(weights)),
        out_specs=vmem,
        scratch_shapes=[
            pltpu.VMEM((parts, lines, cores, rows, width), jnp.bfloat16),
            pltpu.VMEM((parts, 2 * WIDE, depth), jnp.bfloat16),
            pltpu.VMEM((2, rows, depth), jnp.bfloat16),
            pltpu.VMEM((rows, 2 * WIDE), jnp.float32),
            pltpu.VMEM((rows, 1), jnp.float32),
            pltpu.SemaphoreType.DMA((parts, 2)),
            pltpu.SemaphoreType.DMA((parts, 3)),
        ],
        compiler_params=pltpu.CompilerParams(vmem_limit_bytes=56 * 1024 * 1024),
        cost_estimate=pl.CostEstimate(
            flops=4 * rows * WIDE * parts * depth,
            bytes_accessed=2 * parts * depth * (rows + 2 * WIDE),
            transcendentals=2 * rows * WIDE,
        ),
    )(own, gain, meta, *xs, *dep, *weights)


def across(value, turn):
    count = lax.axis_size("section")
    pairs = [(i, i ^ 1) if turn == 0 else (i, count - 1 - i) for i in range(count)]
    return lax.ppermute(value, "section", pairs)


def to_all(value, axis):
    count = lax.axis_size(axis)
    return lax.all_to_all(jnp.broadcast_to(value[None], (count,) + value.shape), axis, 0, 0)


def shards(
    features,
    dw_weight,
    ln_gain,
    ln_bias,
    layer_scale,
    proj_weight,
    text_embed,
    positions,
    rms_gain,
    head_weight,
    labels,
):
    sections = lax.axis_size("section")
    parts = lax.axis_size("dp")
    shard_index = lax.axis_index(("section",) + VOCAB)
    places = positions[0]
    targets = labels[0]
    columns = head_weight.shape[1]
    slots = lax.iota(jnp.int32, targets.shape[0])

    weight = head_weight.T
    low_all = lax.all_gather(weight[:LOW], "dp", axis=0)
    high = jnp.pad(weight[LOW:], ((0, 2 * WIDE - columns), (0, 0)))
    left, right = shifted(high, "dp", -1), shifted(high, "dp", 1)

    text = lax.all_gather(text_embed[0], ("section", "zl"), axis=0)
    is_text = jnp.all(slots[:, None] != places[None, :], axis=1)
    rank = jnp.sum(
        jnp.where((slots[None, :] < slots[:, None]) & is_text[None, :], 1, 0), axis=1
    )
    text_rows = slots.shape[0] - places.shape[0]
    select = (rank[None, :] == lax.iota(jnp.int32, text_rows)[:, None]) & is_text[None, :]
    text_slots = jnp.sum(jnp.where(select, slots[None, :], 0), axis=1)
    image = features[0]
    height, width, chans = image.shape
    above, below = extended(image, VOCAB, 3)
    padded = jnp.concatenate([above, image, below])

    padded = jnp.pad(padded, ((0, 0), (3, 3), (0, 0))).astype(jnp.float32)
    conv = jnp.zeros((height, width, chans), jnp.float32)
    for row_off in range(7):
        for col_off in range(7):
            conv = (
                conv
                + padded[row_off : row_off + height, col_off : col_off + width]
                * dw_weight[row_off, col_off]
            )
    sums = jnp.stack(
        [jnp.sum(conv, axis=-1).reshape(-1), jnp.sum(conv * conv, axis=-1).reshape(-1)]
    )
    sums = lax.psum(sums, "section")
    all_chans = chans * sections
    middle = sums[0].reshape(height, width) / all_chans
    spread = sums[1].reshape(height, width) / all_chans - middle * middle
    normal = (conv - middle[..., None]) * lax.rsqrt(spread + 1e-06)[..., None] * ln_gain + ln_bias
    block = image.astype(jnp.float32) + layer_scale * normal
    pooled = block.reshape(height // 4, 4, width // 4, 4, chans).mean(axis=(1, 3))
    pooled = pooled.reshape(-1, chans).astype(jnp.bfloat16)

    tokens = to_all(pooled, VOCAB)
    rows = jnp.dot(tokens.reshape(-1, chans), proj_weight, preferred_element_type=jnp.float32)
    for turn in range(2):
        rows = rows + across(rows.astype(jnp.bfloat16), turn).astype(jnp.float32)
    rows = rows.astype(jnp.bfloat16)
    text, _ = lax.optimization_barrier((text, rows))
    text = jnp.einsum(
        "jsr,szrc->zjc",
        select.astype(jnp.bfloat16).reshape(text_rows, sections, -1),
        text.reshape((sections, -1) + text.shape[1:]),
        preferred_element_type=jnp.float32,
    ).astype(jnp.bfloat16)
    text_all = lax.all_gather(text, ("y", "core"), axis=0)
    text_all = text_all.reshape((lax.axis_size("y"), lax.axis_size("core")) + text.shape)

    rows, left, right = lax.optimization_barrier((rows, left, right))
    half = high.shape[0] // 2
    far, off = shifted(left[:half], "dp", -1), shifted(right[half:], "dp", 1)
    rows = to_all(rows, "zl")
    early = rows
    rows = to_all(rows, "y")
    rows, text_all, far, off, low_all = lax.optimization_barrier(
        (rows, text_all, far, off, low_all)
    )
    partner = lax.ppermute(rows, "core", [(0, 1), (1, 0)])

    gain = rms_gain.reshape(-1, 1, text_embed.shape[2])
    own = jnp.stack([lax.axis_index("dp"), lax.axis_index("core")])
    offsets = (0, parts - 1, 1, 2)

    def stats(at, xs, dep):
        ids = jnp.sum(jnp.where(at[:, None] == slots[None, :], targets[None, :], 0), axis=1)
        ids = ids - shard_index * columns
        return head_stats(
            own,
            gain,
            jnp.stack([at, ids], axis=1),
            xs,
            (low_all, high, left, right, far, off),
            dep,
            columns,
            offsets,
            targets.shape[0],
        )

    of_text = stats(text_slots, (text_all,), (early,))
    of_visual = stats(places, (rows, partner), ())
    both = (of_text + of_visual)[:3]

    def merged(pieces):
        tops, totals, chosen = pieces[:, 0], pieces[:, 1], pieces[:, 2]
        top = jnp.max(tops, axis=0)
        return jnp.stack(
            [top, jnp.sum(totals * jnp.exp(tops - top), axis=0), jnp.sum(chosen, axis=0)]
        )

    for turn in range(2):
        both = merged(jnp.stack([both, across(both, turn)]))
    both = both.reshape(3, sections, -1)
    both = lax.dynamic_index_in_dim(both, lax.axis_index("section"), 1, keepdims=False)
    top, total, chosen = merged(to_all(both, VOCAB))
    loss = top + jnp.log(total) - chosen
    return (pooled[None], loss[None])


def solution(mesh):
    in_specs = (
        P("dp", VOCAB, None, "section"),
        P(None, None, "section"),
        P("section"),
        P("section"),
        P("section"),
        P("section", VOCAB),
        P("dp", "section", VOCAB),
        P("dp", None),
        P(),
        P("dp", ("section",) + VOCAB),
        P("dp", None),
    )
    out_specs = (P("dp", VOCAB, "section"), P("dp", "section"))
    sizes = (mesh.shape["section"], mesh.shape["vocab"] // 8, 4, 2, mesh.shape["dp"])
    mesh = jax.sharding.Mesh(mesh.devices.reshape(sizes), ("section",) + VOCAB + ("dp",))
    return jax.shard_map(shards, mesh=mesh, in_specs=in_specs, out_specs=out_specs, check_vma=False)
```

```python
import functools

import jax
import jax.numpy as jnp
from jax import lax
from jax.experimental import pallas as pl
from jax.experimental.pallas import tpu as pltpu
from jax.sharding import PartitionSpec as P

WIDE = 256
VOCAB = ("zl", "y", "core")


def shifted(value, axis, step):
    count = lax.axis_size(axis)
    return lax.ppermute(value, axis, [((i + step) % count, i) for i in range(count)])


def extended(cells, axis, width):
    count = lax.axis_size(axis)
    ends = count - 1
    head, tail = cells[:width], cells[-width:]
    above = lax.ppermute(tail, axis, [(i, (i + 1) % count) for i in range(ends)])
    below = lax.ppermute(head, axis, [((i + 1) % count, i) for i in range(ends)])
    return above, below


def head_kernel(columns, offsets, from_text, own_ref, gain_ref, meta_ref, *refs):
    x_v, w_v, scaled, total, squares, sem_x, sem_w = refs[-7:]
    out_ref = refs[-8]
    w_low, w_own, w_left, w_right, w_far, w_off = refs[-14:-8]
    parts, lines, cores, rows, width = x_v.shape
    own, core = own_ref[0], own_ref[1]

    def block(j):
        return lax.rem(own + offsets[j], parts)

    def x_copies(j):
        if from_text:
            return [pltpu.make_async_copy(refs[0].at[block(j)], x_v.at[j], sem_x.at[j, 0])]
        return [
            pltpu.make_async_copy(
                refs[k].at[:, block(j)],
                x_v.at[j, :, core if k == 0 else 1 - core],
                sem_x.at[j, k],
            )
            for k in range(2)
        ]

    def w_copies(j):
        copies = [
            pltpu.make_async_copy(
                w_low.at[block(j)], w_v.at[j, pl.ds(0, WIDE)], sem_w.at[j, 0]
            )
        ]
        if j < 3:
            pieces = ((w_own, w_left, w_right)[j],)
        else:
            pieces = (w_far, w_off)
        size = WIDE // len(pieces)
        for k, piece in enumerate(pieces):
            copies.append(
                pltpu.make_async_copy(
                    piece, w_v.at[j, pl.ds(WIDE + k * size, size)], sem_w.at[j, k + 1]
                )
            )
        return copies

    for j in range(parts):
        for copy in x_copies(j) + w_copies(j):
            copy.start()
    for j in range(parts):
        for copy in x_copies(j):
            copy.wait()
        sums = jnp.zeros((rows, width), jnp.float32)
        for line in range(lines):
            for at in range(cores):
                piece = line * cores + at
                wide = x_v[j, line, at].astype(jnp.float32)
                sums = sums + wide * wide
                gain = gain_ref[block(j) * (lines * cores) + piece]
                scaled[:, piece * width : (piece + 1) * width] = (wide * gain).astype(
                    jnp.bfloat16
                )
        for copy in w_copies(j):
            copy.wait()
        part = lax.dot_general(
            scaled[...], w_v[j], (((1,), (1,)), ((), ())), preferred_element_type=jnp.float32
        )
        sums = jnp.sum(sums, axis=1, keepdims=True)
        if j == 0:
            total[...] = part
            squares[...] = sums
        else:
            total[...] += part
            squares[...] += sums
    factor = lax.rsqrt(squares[...] / (parts * lines * cores * width) + 1e-05)
    logits = total[...] * factor
    at = lax.broadcasted_iota(jnp.int32, logits.shape, 1)
    real = at < columns
    top = jnp.max(jnp.where(real, logits, -jnp.inf), axis=1, keepdims=True)
    summed = jnp.sum(
        jnp.where(real, jnp.exp(logits - top), 0.0), axis=1, keepdims=True
    )
    chosen = jnp.sum(
        jnp.where((at == meta_ref[:, 1:2]) & real, logits, 0.0), axis=1, keepdims=True
    )
    hit = (
        lax.broadcasted_iota(jnp.int32, (rows, out_ref.shape[1]), 1) == meta_ref[:, 0:1]
    )
    out_ref[...] = jnp.zeros(out_ref.shape, jnp.float32)
    for k, value in enumerate((top, summed, chosen)):
        out_ref[k : k + 1, :] = jnp.sum(jnp.where(hit, value, 0.0), axis=0, keepdims=True)


def head_stats(own, gain, meta, xs, weights, dep, columns, offsets, places):
    from_text = len(xs) == 1
    rows = meta.shape[0]
    parts, lines, cores = len(offsets), 4, 2
    width = xs[0].shape[-1]
    depth = lines * cores * width
    vmem = pl.BlockSpec(memory_space=pltpu.VMEM)
    anywhere = pl.BlockSpec(memory_space=pl.ANY)
    return pl.pallas_call(
        functools.partial(head_kernel, columns, offsets, from_text),
        out_shape=jax.ShapeDtypeStruct((8, places), jnp.float32),
        in_specs=[pl.BlockSpec(memory_space=pltpu.SMEM), vmem, vmem]
        + [anywhere] * (len(xs) + len(dep) + len(weights)),
        out_specs=vmem,
        scratch_shapes=[
            pltpu.VMEM((parts, lines, cores, rows, width), jnp.bfloat16),
            pltpu.VMEM((parts, 2 * WIDE, depth), jnp.bfloat16),
            pltpu.VMEM((rows, depth), jnp.bfloat16),
            pltpu.VMEM((rows, 2 * WIDE), jnp.float32),
            pltpu.VMEM((rows, 1), jnp.float32),
            pltpu.SemaphoreType.DMA((parts, 2)),
            pltpu.SemaphoreType.DMA((parts, 3)),
        ],
        compiler_params=pltpu.CompilerParams(vmem_limit_bytes=56 * 1024 * 1024),
        cost_estimate=pl.CostEstimate(
            flops=4 * rows * WIDE * parts * depth,
            bytes_accessed=2 * parts * depth * (rows + 2 * WIDE),
            transcendentals=2 * rows * WIDE,
        ),
    )(own, gain, meta, *xs, *dep, *weights)


def across(value, turn):
    count = lax.axis_size("section")
    pairs = [(i, i ^ 1) if turn == 0 else (i, count - 1 - i) for i in range(count)]
    return lax.ppermute(value, "section", pairs)


def to_all(value, axis):
    count = lax.axis_size(axis)
    return lax.all_to_all(jnp.broadcast_to(value[None], (count,) + value.shape), axis, 0, 0)


def shards(
    features,
    dw_weight,
    ln_gain,
    ln_bias,
    layer_scale,
    proj_weight,
    text_embed,
    positions,
    rms_gain,
    head_weight,
    labels,
):
    sections = lax.axis_size("section")
    parts = lax.axis_size("dp")
    shard_index = lax.axis_index(("section",) + VOCAB)
    places = positions[0]
    targets = labels[0]
    columns = head_weight.shape[1]
    slots = lax.iota(jnp.int32, targets.shape[0])

    weight = head_weight.T
    low_all = lax.all_gather(weight[:WIDE], "dp", axis=0)
    high = jnp.pad(weight[WIDE:], ((0, 2 * WIDE - columns), (0, 0)))
    left, right = shifted(high, "dp", -1), shifted(high, "dp", 1)

    text = to_all(text_embed[0], "section")

    image = features[0]
    height, width, chans = image.shape
    above, below = extended(image, VOCAB, 3)
    padded = jnp.concatenate([above, image, below])

    padded = jnp.pad(padded, ((0, 0), (3, 3), (0, 0))).astype(jnp.float32)
    conv = jnp.zeros((height, width, chans), jnp.float32)
    for row_off in range(7):
        for col_off in range(7):
            conv = (
                conv
                + padded[row_off : row_off + height, col_off : col_off + width]
                * dw_weight[row_off, col_off]
            )
    sums = jnp.stack(
        [jnp.sum(conv, axis=-1).reshape(-1), jnp.sum(conv * conv, axis=-1).reshape(-1)]
    )
    sums, text = lax.optimization_barrier((sums, text))
    sums = lax.psum(sums, "section")
    all_chans = chans * sections
    middle = sums[0].reshape(height, width) / all_chans
    spread = sums[1].reshape(height, width) / all_chans - middle * middle
    normal = (conv - middle[..., None]) * lax.rsqrt(spread + 1e-06)[..., None] * ln_gain + ln_bias
    block = image.astype(jnp.float32) + layer_scale * normal
    pooled = block.reshape(height // 4, 4, width // 4, 4, chans).mean(axis=(1, 3))
    pooled = pooled.reshape(-1, chans).astype(jnp.bfloat16)

    tokens = to_all(pooled, VOCAB)
    rows = jnp.dot(tokens.reshape(-1, chans), proj_weight, preferred_element_type=jnp.float32)
    for turn in range(2):
        rows = rows + across(rows.astype(jnp.bfloat16), turn).astype(jnp.float32)
    rows = rows.astype(jnp.bfloat16)

    is_text = jnp.all(slots[:, None] != places[None, :], axis=1)
    rank = jnp.sum(
        jnp.where((slots[None, :] < slots[:, None]) & is_text[None, :], 1, 0), axis=1
    )
    text_rows = slots.shape[0] - places.shape[0]
    select = (rank[None, :] == lax.iota(jnp.int32, text_rows)[:, None]) & is_text[None, :]
    text, _, _ = lax.optimization_barrier((text, tokens, low_all))
    text = jnp.dot(
        select.astype(jnp.bfloat16),
        text.reshape(slots.shape[0], -1),
        preferred_element_type=jnp.float32,
    ).astype(jnp.bfloat16)
    text_slots = jnp.sum(jnp.where(select, slots[None, :], 0), axis=1)
    text_all = lax.all_gather(text, VOCAB, axis=0)
    text_all = text_all.reshape(tuple(lax.axis_size(axis) for axis in VOCAB) + text.shape)

    rows, left, right = lax.optimization_barrier((rows, left, right))
    half = WIDE // 2
    far, off = shifted(left[:half], "dp", -1), shifted(right[half:], "dp", 1)
    rows = to_all(rows, "zl")
    early = rows
    rows = to_all(rows, "y")
    rows, text_all, far, off = lax.optimization_barrier((rows, text_all, far, off))
    partner = lax.ppermute(rows, "core", [(0, 1), (1, 0)])

    gain = rms_gain.reshape(-1, 1, text.shape[1])
    own = jnp.stack([lax.axis_index("dp"), lax.axis_index("core")])
    offsets = (0, parts - 1, 1, 2)

    def stats(at, xs, dep):
        ids = jnp.sum(jnp.where(at[:, None] == slots[None, :], targets[None, :], 0), axis=1)
        ids = ids - shard_index * columns
        return head_stats(
            own,
            gain,
            jnp.stack([at, ids], axis=1),
            xs,
            (low_all, high, left, right, far, off),
            dep,
            columns,
            offsets,
            targets.shape[0],
        )

    of_text = stats(text_slots, (text_all,), (early,))
    of_visual = stats(places, (rows, partner), ())
    both = (of_text + of_visual)[:3]

    def merged(pieces):
        tops, totals, chosen = pieces[:, 0], pieces[:, 1], pieces[:, 2]
        top = jnp.max(tops, axis=0)
        return jnp.stack(
            [top, jnp.sum(totals * jnp.exp(tops - top), axis=0), jnp.sum(chosen, axis=0)]
        )

    for turn in range(2):
        both = merged(jnp.stack([both, across(both, turn)]))
    both = both.reshape(3, sections, -1)
    both = lax.dynamic_index_in_dim(both, lax.axis_index("section"), 1, keepdims=False)
    top, total, chosen = merged(to_all(both, VOCAB))
    loss = top + jnp.log(total) - chosen
    return (pooled[None], loss[None])


def solution(mesh):
    in_specs = (
        P("dp", VOCAB, None, "section"),
        P(None, None, "section"),
        P("section"),
        P("section"),
        P("section"),
        P("section", VOCAB),
        P("dp", "section", VOCAB),
        P("dp", None),
        P(),
        P("dp", ("section",) + VOCAB),
        P("dp", None),
    )
    out_specs = (P("dp", VOCAB, "section"), P("dp", "section"))
    sizes = (mesh.shape["section"], mesh.shape["vocab"] // 8, 4, 2, mesh.shape["dp"])
    mesh = jax.sharding.Mesh(mesh.devices.reshape(sizes), ("section",) + VOCAB + ("dp",))
    return jax.shard_map(shards, mesh=mesh, in_specs=in_specs, out_specs=out_specs, check_vma=False)
```

```python
import functools

import jax
import jax.numpy as jnp
from jax import lax
from jax.experimental import pallas as pl
from jax.experimental.pallas import tpu as pltpu
from jax.sharding import PartitionSpec as P

WIDE = 256
LOW = 128
VOCAB = ("zl", "y", "core")


def shifted(value, axis, step):
    count = lax.axis_size(axis)
    return lax.ppermute(value, axis, [((i + step) % count, i) for i in range(count)])


def extended(cells, axis, width):
    count = lax.axis_size(axis)
    ends = count - 1
    head, tail = cells[:width], cells[-width:]
    return jnp.concatenate(
        [
            lax.ppermute(tail, axis, [(i, (i + 1) % count) for i in range(ends)]),
            cells,
            lax.ppermute(head, axis, [((i + 1) % count, i) for i in range(ends)]),
        ],
        axis=0,
    )


def head_kernel(columns, offsets, from_text, own_ref, gain_ref, meta_ref, *refs):
    x_v, w_v, scaled, total, squares, sem_x, sem_w = refs[-7:]
    out_ref = refs[-8]
    w_low, w_own, w_left, w_right, w_far, w_off = refs[-14:-8]
    parts, lines, cores, rows, width = x_v.shape
    own, core = own_ref[0], own_ref[1]

    def block(j):
        return lax.rem(own + offsets[j], parts)

    def x_copies(j):
        if from_text:
            return [pltpu.make_async_copy(refs[0].at[block(j)], x_v.at[j], sem_x.at[j, 0])]
        return [
            pltpu.make_async_copy(
                refs[k].at[:, block(j)],
                x_v.at[j, :, core if k == 0 else 1 - core],
                sem_x.at[j, k],
            )
            for k in range(2)
        ]

    def w_copies(j):
        copies = [
            pltpu.make_async_copy(
                w_low.at[block(j)], w_v.at[j, pl.ds(0, LOW)], sem_w.at[j, 0]
            )
        ]
        if j < 3:
            pieces = ((w_own, w_left, w_right)[j],)
        else:
            pieces = (w_far, w_off)
        size = (2 * WIDE - LOW) // len(pieces)
        for k, piece in enumerate(pieces):
            copies.append(
                pltpu.make_async_copy(
                    piece, w_v.at[j, pl.ds(LOW + k * size, size)], sem_w.at[j, k + 1]
                )
            )
        return copies

    for j in range(parts):
        for copy in x_copies(j) + w_copies(j):
            copy.start()
    for j in range(parts):
        for copy in x_copies(j):
            copy.wait()
        sums = jnp.zeros((rows, width), jnp.float32)
        for line in range(lines):
            for at in range(cores):
                piece = line * cores + at
                wide = x_v[j, line, at].astype(jnp.float32)
                sums = sums + wide * wide
                gain = gain_ref[block(j) * (lines * cores) + piece]
                scaled[:, piece * width : (piece + 1) * width] = (wide * gain).astype(
                    jnp.bfloat16
                )
        for copy in w_copies(j):
            copy.wait()
        part = lax.dot_general(
            scaled[...], w_v[j], (((1,), (1,)), ((), ())), preferred_element_type=jnp.float32
        )
        sums = jnp.sum(sums, axis=1, keepdims=True)
        if j == 0:
            total[...] = part
            squares[...] = sums
        else:
            total[...] += part
            squares[...] += sums
    factor = lax.rsqrt(squares[...] / (parts * lines * cores * width) + 1e-05)
    logits = total[...] * factor
    at = lax.broadcasted_iota(jnp.int32, logits.shape, 1)
    real = at < columns
    top = jnp.max(jnp.where(real, logits, -jnp.inf), axis=1, keepdims=True)
    summed = jnp.sum(
        jnp.where(real, jnp.exp(logits - top), 0.0), axis=1, keepdims=True
    )
    chosen = jnp.sum(
        jnp.where((at == meta_ref[:, 1:2]) & real, logits, 0.0), axis=1, keepdims=True
    )
    hit = (
        lax.broadcasted_iota(jnp.int32, (rows, out_ref.shape[1]), 1) == meta_ref[:, 0:1]
    )
    out_ref[...] = jnp.zeros(out_ref.shape, jnp.float32)
    for k, value in enumerate((top, summed, chosen)):
        out_ref[k : k + 1, :] = jnp.sum(jnp.where(hit, value, 0.0), axis=0, keepdims=True)


def head_stats(own, gain, meta, xs, weights, dep, columns, offsets, places):
    from_text = len(xs) == 1
    rows = meta.shape[0]
    parts, lines, cores = len(offsets), 4, 2
    width = xs[0].shape[-1]
    depth = lines * cores * width
    vmem = pl.BlockSpec(memory_space=pltpu.VMEM)
    anywhere = pl.BlockSpec(memory_space=pl.ANY)
    return pl.pallas_call(
        functools.partial(head_kernel, columns, offsets, from_text),
        out_shape=jax.ShapeDtypeStruct((8, places), jnp.float32),
        in_specs=[pl.BlockSpec(memory_space=pltpu.SMEM), vmem, vmem]
        + [anywhere] * (len(xs) + len(dep) + len(weights)),
        out_specs=vmem,
        scratch_shapes=[
            pltpu.VMEM((parts, lines, cores, rows, width), jnp.bfloat16),
            pltpu.VMEM((parts, 2 * WIDE, depth), jnp.bfloat16),
            pltpu.VMEM((rows, depth), jnp.bfloat16),
            pltpu.VMEM((rows, 2 * WIDE), jnp.float32),
            pltpu.VMEM((rows, 1), jnp.float32),
            pltpu.SemaphoreType.DMA((parts, 2)),
            pltpu.SemaphoreType.DMA((parts, 3)),
        ],
        compiler_params=pltpu.CompilerParams(vmem_limit_bytes=56 * 1024 * 1024),
        cost_estimate=pl.CostEstimate(
            flops=4 * rows * WIDE * parts * depth,
            bytes_accessed=2 * parts * depth * (rows + 2 * WIDE),
            transcendentals=2 * rows * WIDE,
        ),
    )(own, gain, meta, *xs, *dep, *weights)


def across(value, turn):
    count = lax.axis_size("section")
    pairs = [(i, i ^ 1) if turn == 0 else (i, count - 1 - i) for i in range(count)]
    return lax.ppermute(value, "section", pairs)


def to_all(value, axis):
    count = lax.axis_size(axis)
    return lax.all_to_all(jnp.broadcast_to(value[None], (count,) + value.shape), axis, 0, 0)


def shards(
    features,
    dw_weight,
    ln_gain,
    ln_bias,
    layer_scale,
    proj_weight,
    text_embed,
    positions,
    rms_gain,
    head_weight,
    labels,
):
    sections = lax.axis_size("section")
    parts = lax.axis_size("dp")
    shard_index = lax.axis_index(("section",) + VOCAB)
    places = positions[0]
    targets = labels[0]
    columns = head_weight.shape[1]
    slots = lax.iota(jnp.int32, targets.shape[0])

    text = to_all(text_embed[0], "section").reshape(slots.shape[0], -1)

    weight = head_weight.T
    low_all = lax.all_gather(weight[:LOW], "dp", axis=0)
    high = jnp.pad(weight[LOW:], ((0, 2 * WIDE - columns), (0, 0)))
    left, right = shifted(high, "dp", -1), shifted(high, "dp", 1)

    image = features[0]
    height, width, chans = image.shape
    padded = extended(image, VOCAB, 3)
    padded = jnp.pad(padded, ((0, 0), (3, 3), (0, 0))).astype(jnp.float32)
    conv = jnp.zeros((height, width, chans), jnp.float32)
    for row_off in range(7):
        for col_off in range(7):
            conv = (
                conv
                + padded[row_off : row_off + height, col_off : col_off + width]
                * dw_weight[row_off, col_off]
            )
    sums = jnp.stack(
        [jnp.sum(conv, axis=-1).reshape(-1), jnp.sum(conv * conv, axis=-1).reshape(-1)]
    )
    sums = lax.psum(sums, "section")

    is_text = jnp.all(slots[:, None] != places[None, :], axis=1)
    rank = jnp.sum(
        jnp.where((slots[None, :] < slots[:, None]) & is_text[None, :], 1, 0), axis=1
    )
    text_rows = slots.shape[0] - places.shape[0]
    select = (rank[None, :] == lax.iota(jnp.int32, text_rows)[:, None]) & is_text[None, :]
    text, _ = lax.optimization_barrier((text, sums))
    text = jnp.dot(
        select.astype(jnp.bfloat16), text, preferred_element_type=jnp.float32
    ).astype(jnp.bfloat16)
    text_slots = jnp.sum(jnp.where(select, slots[None, :], 0), axis=1)
    text_all = lax.all_gather(text, VOCAB, axis=0)
    text_all = text_all.reshape(tuple(lax.axis_size(axis) for axis in VOCAB) + text.shape)
    all_chans = chans * sections
    middle = sums[0].reshape(height, width) / all_chans
    spread = sums[1].reshape(height, width) / all_chans - middle * middle
    normal = (conv - middle[..., None]) * lax.rsqrt(spread + 1e-06)[..., None] * ln_gain + ln_bias
    block = image.astype(jnp.float32) + layer_scale * normal
    pooled = block.reshape(height // 4, 4, width // 4, 4, chans).mean(axis=(1, 3))
    pooled = pooled.reshape(-1, chans).astype(jnp.bfloat16)

    tokens = to_all(pooled, VOCAB).reshape(-1, chans)
    rows = jnp.dot(tokens, proj_weight, preferred_element_type=jnp.float32)
    for turn in range(2):
        rows = rows + across(rows.astype(jnp.bfloat16), turn).astype(jnp.float32)
    rows = rows.astype(jnp.bfloat16)

    rows, left, right = lax.optimization_barrier((rows, left, right))
    half = high.shape[0] // 2
    far, off = shifted(left[:half], "dp", -1), shifted(right[half:], "dp", 1)
    rows = to_all(rows, "zl")
    rows, text_all = lax.optimization_barrier((rows, text_all))
    early = rows
    rows = to_all(rows, "y")
    rows, far, off, low_all = lax.optimization_barrier((rows, far, off, low_all))
    partner = lax.ppermute(rows, "core", [(0, 1), (1, 0)])

    gain = rms_gain.reshape(-1, 1, text.shape[1])
    own = jnp.stack([lax.axis_index("dp"), lax.axis_index("core")])
    offsets = (0, parts - 1, 1, 2)

    def stats(at, xs, dep):
        ids = jnp.sum(jnp.where(at[:, None] == slots[None, :], targets[None, :], 0), axis=1)
        ids = ids - shard_index * columns
        return head_stats(
            own,
            gain,
            jnp.stack([at, ids], axis=1),
            xs,
            (low_all, high, left, right, far, off),
            dep,
            columns,
            offsets,
            targets.shape[0],
        )

    of_text = stats(text_slots, (text_all,), (early,))
    of_visual = stats(places, (rows, partner), ())
    both = (of_text + of_visual)[:3]

    def merged(pieces):
        tops, totals, chosen = pieces[:, 0], pieces[:, 1], pieces[:, 2]
        top = jnp.max(tops, axis=0)
        return jnp.stack(
            [top, jnp.sum(totals * jnp.exp(tops - top), axis=0), jnp.sum(chosen, axis=0)]
        )

    for turn in range(2):
        both = merged(jnp.stack([both, across(both, turn)]))
    both = both.reshape(3, sections, -1)
    both = lax.dynamic_index_in_dim(both, lax.axis_index("section"), 1, keepdims=False)
    top, total, chosen = merged(to_all(both, VOCAB))
    loss = top + jnp.log(total) - chosen
    return (pooled[None], loss[None])


def solution(mesh):
    in_specs = (
        P("dp", VOCAB, None, "section"),
        P(None, None, "section"),
        P("section"),
        P("section"),
        P("section"),
        P("section", VOCAB),
        P("dp", "section", VOCAB),
        P("dp", None),
        P(),
        P("dp", ("section",) + VOCAB),
        P("dp", None),
    )
    out_specs = (P("dp", VOCAB, "section"), P("dp", "section"))
    sizes = (mesh.shape["section"], mesh.shape["vocab"] // 8, 4, 2, mesh.shape["dp"])
    mesh = jax.sharding.Mesh(mesh.devices.reshape(sizes), ("section",) + VOCAB + ("dp",))
    return jax.shard_map(shards, mesh=mesh, in_specs=in_specs, out_specs=out_specs, check_vma=False)
```

```python
import functools

import jax
import jax.numpy as jnp
from jax import lax
from jax.experimental import pallas as pl
from jax.experimental.pallas import tpu as pltpu
from jax.sharding import PartitionSpec as P

WIDE = 256
LOW = 160
VOCAB = ("zl", "y", "core")


def shifted(value, axis, step):
    count = lax.axis_size(axis)
    return lax.ppermute(value, axis, [((i + step) % count, i) for i in range(count)])


def extended(cells, axis, width):
    count = lax.axis_size(axis)
    ends = count - 1
    head, tail = cells[:width], cells[-width:]
    return jnp.concatenate(
        [
            lax.ppermute(tail, axis, [(i, (i + 1) % count) for i in range(ends)]),
            cells,
            lax.ppermute(head, axis, [((i + 1) % count, i) for i in range(ends)]),
        ],
        axis=0,
    )


def head_kernel(columns, offsets, from_text, own_ref, gain_ref, meta_ref, *refs):
    x_v, w_v, scaled, total, squares, sem_x, sem_w = refs[-7:]
    out_ref = refs[-8]
    w_low, w_own, w_left, w_right, w_far, w_off = refs[-14:-8]
    parts, lines, cores, rows, width = x_v.shape
    own, core = own_ref[0], own_ref[1]

    def block(j):
        return lax.rem(own + offsets[j], parts)

    def x_copies(j):
        if from_text:
            return [pltpu.make_async_copy(refs[0].at[block(j)], x_v.at[j], sem_x.at[j, 0])]
        return [
            pltpu.make_async_copy(
                refs[k].at[:, block(j)],
                x_v.at[j, :, core if k == 0 else 1 - core],
                sem_x.at[j, k],
            )
            for k in range(2)
        ]

    def w_copies(j):
        copies = [
            pltpu.make_async_copy(
                w_low.at[block(j)], w_v.at[j, pl.ds(0, LOW)], sem_w.at[j, 0]
            )
        ]
        if j < 3:
            pieces = ((w_own, w_left, w_right)[j],)
        else:
            pieces = (w_far, w_off)
        size = (2 * WIDE - LOW) // len(pieces)
        for k, piece in enumerate(pieces):
            copies.append(
                pltpu.make_async_copy(
                    piece, w_v.at[j, pl.ds(LOW + k * size, size)], sem_w.at[j, k + 1]
                )
            )
        return copies

    for j in range(parts):
        for copy in x_copies(j) + w_copies(j):
            copy.start()
    for j in range(parts):
        for copy in x_copies(j):
            copy.wait()
        sums = jnp.zeros((rows, width), jnp.float32)
        for line in range(lines):
            for at in range(cores):
                piece = line * cores + at
                wide = x_v[j, line, at].astype(jnp.float32)
                sums = sums + wide * wide
                gain = gain_ref[block(j) * (lines * cores) + piece]
                scaled[:, piece * width : (piece + 1) * width] = (wide * gain).astype(
                    jnp.bfloat16
                )
        for copy in w_copies(j):
            copy.wait()
        part = lax.dot_general(
            scaled[...], w_v[j], (((1,), (1,)), ((), ())), preferred_element_type=jnp.float32
        )
        sums = jnp.sum(sums, axis=1, keepdims=True)
        if j == 0:
            total[...] = part
            squares[...] = sums
        else:
            total[...] += part
            squares[...] += sums
    factor = lax.rsqrt(squares[...] / (parts * lines * cores * width) + 1e-05)
    logits = total[...] * factor
    at = lax.broadcasted_iota(jnp.int32, logits.shape, 1)
    real = at < columns
    top = jnp.max(jnp.where(real, logits, -jnp.inf), axis=1, keepdims=True)
    summed = jnp.sum(
        jnp.where(real, jnp.exp(logits - top), 0.0), axis=1, keepdims=True
    )
    chosen = jnp.sum(
        jnp.where((at == meta_ref[:, 1:2]) & real, logits, 0.0), axis=1, keepdims=True
    )
    hit = (
        lax.broadcasted_iota(jnp.int32, (rows, out_ref.shape[1]), 1) == meta_ref[:, 0:1]
    )
    out_ref[...] = jnp.zeros(out_ref.shape, jnp.float32)
    for k, value in enumerate((top, summed, chosen)):
        out_ref[k : k + 1, :] = jnp.sum(jnp.where(hit, value, 0.0), axis=0, keepdims=True)


def head_stats(own, gain, meta, xs, weights, dep, columns, offsets, places):
    from_text = len(xs) == 1
    rows = meta.shape[0]
    parts, lines, cores = len(offsets), 4, 2
    width = xs[0].shape[-1]
    depth = lines * cores * width
    vmem = pl.BlockSpec(memory_space=pltpu.VMEM)
    anywhere = pl.BlockSpec(memory_space=pl.ANY)
    return pl.pallas_call(
        functools.partial(head_kernel, columns, offsets, from_text),
        out_shape=jax.ShapeDtypeStruct((8, places), jnp.float32),
        in_specs=[pl.BlockSpec(memory_space=pltpu.SMEM), vmem, vmem]
        + [anywhere] * (len(xs) + len(dep) + len(weights)),
        out_specs=vmem,
        scratch_shapes=[
            pltpu.VMEM((parts, lines, cores, rows, width), jnp.bfloat16),
            pltpu.VMEM((parts, 2 * WIDE, depth), jnp.bfloat16),
            pltpu.VMEM((rows, depth), jnp.bfloat16),
            pltpu.VMEM((rows, 2 * WIDE), jnp.float32),
            pltpu.VMEM((rows, 1), jnp.float32),
            pltpu.SemaphoreType.DMA((parts, 2)),
            pltpu.SemaphoreType.DMA((parts, 3)),
        ],
        compiler_params=pltpu.CompilerParams(vmem_limit_bytes=56 * 1024 * 1024),
        cost_estimate=pl.CostEstimate(
            flops=4 * rows * WIDE * parts * depth,
            bytes_accessed=2 * parts * depth * (rows + 2 * WIDE),
            transcendentals=2 * rows * WIDE,
        ),
    )(own, gain, meta, *xs, *dep, *weights)


def across(value, turn):
    count = lax.axis_size("section")
    pairs = [(i, i ^ 1) if turn == 0 else (i, count - 1 - i) for i in range(count)]
    return lax.ppermute(value, "section", pairs)


def to_all(value, axis):
    count = lax.axis_size(axis)
    return lax.all_to_all(jnp.broadcast_to(value[None], (count,) + value.shape), axis, 0, 0)


def shards(
    features,
    dw_weight,
    ln_gain,
    ln_bias,
    layer_scale,
    proj_weight,
    text_embed,
    positions,
    rms_gain,
    head_weight,
    labels,
):
    sections = lax.axis_size("section")
    parts = lax.axis_size("dp")
    shard_index = lax.axis_index(("section",) + VOCAB)
    places = positions[0]
    targets = labels[0]
    columns = head_weight.shape[1]
    slots = lax.iota(jnp.int32, targets.shape[0])

    text = to_all(text_embed[0], "section").reshape(slots.shape[0], -1)

    weight = head_weight.T
    low_all = lax.all_gather(weight[:LOW], "dp", axis=0)
    high = jnp.pad(weight[LOW:], ((0, 2 * WIDE - columns), (0, 0)))
    left, right = shifted(high, "dp", -1), shifted(high, "dp", 1)

    image = features[0]
    height, width, chans = image.shape
    padded = extended(image, VOCAB, 3)
    padded = jnp.pad(padded, ((0, 0), (3, 3), (0, 0))).astype(jnp.float32)
    conv = jnp.zeros((height, width, chans), jnp.float32)
    for row_off in range(7):
        for col_off in range(7):
            conv = (
                conv
                + padded[row_off : row_off + height, col_off : col_off + width]
                * dw_weight[row_off, col_off]
            )
    sums = jnp.stack(
        [jnp.sum(conv, axis=-1).reshape(-1), jnp.sum(conv * conv, axis=-1).reshape(-1)]
    )
    sums = lax.psum(sums, "section")

    is_text = jnp.all(slots[:, None] != places[None, :], axis=1)
    rank = jnp.sum(
        jnp.where((slots[None, :] < slots[:, None]) & is_text[None, :], 1, 0), axis=1
    )
    text_rows = slots.shape[0] - places.shape[0]
    select = (rank[None, :] == lax.iota(jnp.int32, text_rows)[:, None]) & is_text[None, :]
    text, _, _ = lax.optimization_barrier((text, sums, low_all))
    text = jnp.dot(
        select.astype(jnp.bfloat16), text, preferred_element_type=jnp.float32
    ).astype(jnp.bfloat16)
    text_slots = jnp.sum(jnp.where(select, slots[None, :], 0), axis=1)
    text_all = lax.all_gather(text, VOCAB, axis=0)
    text_all = text_all.reshape(tuple(lax.axis_size(axis) for axis in VOCAB) + text.shape)
    all_chans = chans * sections
    middle = sums[0].reshape(height, width) / all_chans
    spread = sums[1].reshape(height, width) / all_chans - middle * middle
    normal = (conv - middle[..., None]) * lax.rsqrt(spread + 1e-06)[..., None] * ln_gain + ln_bias
    block = image.astype(jnp.float32) + layer_scale * normal
    pooled = block.reshape(height // 4, 4, width // 4, 4, chans).mean(axis=(1, 3))
    pooled = pooled.reshape(-1, chans).astype(jnp.bfloat16)

    tokens = to_all(pooled, VOCAB).reshape(-1, chans)
    rows = jnp.dot(tokens, proj_weight, preferred_element_type=jnp.float32)
    for turn in range(2):
        rows = rows + across(rows.astype(jnp.bfloat16), turn).astype(jnp.float32)
    rows = rows.astype(jnp.bfloat16)

    rows, left, right = lax.optimization_barrier((rows, left, right))
    half = high.shape[0] // 2
    far, off = shifted(left[:half], "dp", -1), shifted(right[half:], "dp", 1)
    rows = to_all(rows, "zl")
    rows, text_all = lax.optimization_barrier((rows, text_all))
    early = rows
    rows = to_all(rows, "y")
    rows, far, off, low_all = lax.optimization_barrier((rows, far, off, low_all))
    partner = lax.ppermute(rows, "core", [(0, 1), (1, 0)])

    gain = rms_gain.reshape(-1, 1, text.shape[1])
    own = jnp.stack([lax.axis_index("dp"), lax.axis_index("core")])
    offsets = (0, parts - 1, 1, 2)

    def stats(at, xs, dep):
        ids = jnp.sum(jnp.where(at[:, None] == slots[None, :], targets[None, :], 0), axis=1)
        ids = ids - shard_index * columns
        return head_stats(
            own,
            gain,
            jnp.stack([at, ids], axis=1),
            xs,
            (low_all, high, left, right, far, off),
            dep,
            columns,
            offsets,
            targets.shape[0],
        )

    of_text = stats(text_slots, (text_all,), (early,))
    of_visual = stats(places, (rows, partner), ())
    both = (of_text + of_visual)[:3]

    def merged(pieces):
        tops, totals, chosen = pieces[:, 0], pieces[:, 1], pieces[:, 2]
        top = jnp.max(tops, axis=0)
        return jnp.stack(
            [top, jnp.sum(totals * jnp.exp(tops - top), axis=0), jnp.sum(chosen, axis=0)]
        )

    for turn in range(2):
        both = merged(jnp.stack([both, across(both, turn)]))
    both = both.reshape(3, sections, -1)
    both = lax.dynamic_index_in_dim(both, lax.axis_index("section"), 1, keepdims=False)
    top, total, chosen = merged(to_all(both, VOCAB))
    loss = top + jnp.log(total) - chosen
    return (pooled[None], loss[None])


def solution(mesh):
    in_specs = (
        P("dp", VOCAB, None, "section"),
        P(None, None, "section"),
        P("section"),
        P("section"),
        P("section"),
        P("section", VOCAB),
        P("dp", "section", VOCAB),
        P("dp", None),
        P(),
        P("dp", ("section",) + VOCAB),
        P("dp", None),
    )
    out_specs = (P("dp", VOCAB, "section"), P("dp", "section"))
    sizes = (mesh.shape["section"], mesh.shape["vocab"] // 8, 4, 2, mesh.shape["dp"])
    mesh = jax.sharding.Mesh(mesh.devices.reshape(sizes), ("section",) + VOCAB + ("dp",))
    return jax.shard_map(shards, mesh=mesh, in_specs=in_specs, out_specs=out_specs, check_vma=False)
```

```python
import functools

import jax
import jax.numpy as jnp
from jax import lax
from jax.experimental import pallas as pl
from jax.experimental.pallas import tpu as pltpu
from jax.sharding import PartitionSpec as P

WIDE = 256
LOW = 128
VOCAB = ("zl", "y", "core")


def shifted(value, axis, step):
    count = lax.axis_size(axis)
    return lax.ppermute(value, axis, [((i + step) % count, i) for i in range(count)])


def extended(cells, axis, width):
    count = lax.axis_size(axis)
    ends = count - 1
    head, tail = cells[:width], cells[-width:]
    return jnp.concatenate(
        [
            lax.ppermute(tail, axis, [(i, (i + 1) % count) for i in range(ends)]),
            cells,
            lax.ppermute(head, axis, [((i + 1) % count, i) for i in range(ends)]),
        ],
        axis=0,
    )


def head_kernel(columns, offsets, from_text, own_ref, gain_ref, meta_ref, *refs):
    x_v, w_v, scaled, total, squares, sem_x, sem_w = refs[-7:]
    out_ref = refs[-8]
    w_low, w_own, w_left, w_right, w_far, w_off = refs[-14:-8]
    parts, lines, cores, rows, width = x_v.shape
    own, core = own_ref[0], own_ref[1]

    def block(j):
        return lax.rem(own + offsets[j], parts)

    def x_copies(j):
        if from_text:
            return [pltpu.make_async_copy(refs[0].at[block(j)], x_v.at[j], sem_x.at[j, 0])]
        return [
            pltpu.make_async_copy(
                refs[k].at[:, block(j)],
                x_v.at[j, :, core if k == 0 else 1 - core],
                sem_x.at[j, k],
            )
            for k in range(2)
        ]

    def w_copies(j):
        copies = [
            pltpu.make_async_copy(
                w_low.at[block(j)], w_v.at[j, pl.ds(0, LOW)], sem_w.at[j, 0]
            )
        ]
        if j < 3:
            pieces = ((w_own, w_left, w_right)[j],)
        else:
            pieces = (w_far, w_off)
        size = (2 * WIDE - LOW) // len(pieces)
        for k, piece in enumerate(pieces):
            copies.append(
                pltpu.make_async_copy(
                    piece, w_v.at[j, pl.ds(LOW + k * size, size)], sem_w.at[j, k + 1]
                )
            )
        return copies

    for j in range(parts):
        for copy in x_copies(j) + w_copies(j):
            copy.start()
    for j in range(parts):
        for copy in x_copies(j):
            copy.wait()
        sums = jnp.zeros((rows, width), jnp.float32)
        for line in range(lines):
            for at in range(cores):
                piece = line * cores + at
                wide = x_v[j, line, at].astype(jnp.float32)
                sums = sums + wide * wide
                gain = gain_ref[block(j) * (lines * cores) + piece]
                scaled[:, piece * width : (piece + 1) * width] = (wide * gain).astype(
                    jnp.bfloat16
                )
        for copy in w_copies(j):
            copy.wait()
        part = lax.dot_general(
            scaled[...], w_v[j], (((1,), (1,)), ((), ())), preferred_element_type=jnp.float32
        )
        sums = jnp.sum(sums, axis=1, keepdims=True)
        if j == 0:
            total[...] = part
            squares[...] = sums
        else:
            total[...] += part
            squares[...] += sums
    factor = lax.rsqrt(squares[...] / (parts * lines * cores * width) + 1e-05)
    logits = total[...] * factor
    at = lax.broadcasted_iota(jnp.int32, logits.shape, 1)
    real = at < columns
    top = jnp.max(jnp.where(real, logits, -jnp.inf), axis=1, keepdims=True)
    summed = jnp.sum(
        jnp.where(real, jnp.exp(logits - top), 0.0), axis=1, keepdims=True
    )
    chosen = jnp.sum(
        jnp.where((at == meta_ref[:, 1:2]) & real, logits, 0.0), axis=1, keepdims=True
    )
    hit = (
        lax.broadcasted_iota(jnp.int32, (rows, out_ref.shape[1]), 1) == meta_ref[:, 0:1]
    )
    out_ref[...] = jnp.zeros(out_ref.shape, jnp.float32)
    for k, value in enumerate((top, summed, chosen)):
        out_ref[k : k + 1, :] = jnp.sum(jnp.where(hit, value, 0.0), axis=0, keepdims=True)


def head_stats(own, gain, meta, xs, weights, dep, columns, offsets, places):
    from_text = len(xs) == 1
    rows = meta.shape[0]
    parts, lines, cores = len(offsets), 4, 2
    width = xs[0].shape[-1]
    depth = lines * cores * width
    vmem = pl.BlockSpec(memory_space=pltpu.VMEM)
    anywhere = pl.BlockSpec(memory_space=pl.ANY)
    return pl.pallas_call(
        functools.partial(head_kernel, columns, offsets, from_text),
        out_shape=jax.ShapeDtypeStruct((8, places), jnp.float32),
        in_specs=[pl.BlockSpec(memory_space=pltpu.SMEM), vmem, vmem]
        + [anywhere] * (len(xs) + len(dep) + len(weights)),
        out_specs=vmem,
        scratch_shapes=[
            pltpu.VMEM((parts, lines, cores, rows, width), jnp.bfloat16),
            pltpu.VMEM((parts, 2 * WIDE, depth), jnp.bfloat16),
            pltpu.VMEM((rows, depth), jnp.bfloat16),
            pltpu.VMEM((rows, 2 * WIDE), jnp.float32),
            pltpu.VMEM((rows, 1), jnp.float32),
            pltpu.SemaphoreType.DMA((parts, 2)),
            pltpu.SemaphoreType.DMA((parts, 3)),
        ],
        compiler_params=pltpu.CompilerParams(vmem_limit_bytes=56 * 1024 * 1024),
        cost_estimate=pl.CostEstimate(
            flops=4 * rows * WIDE * parts * depth,
            bytes_accessed=2 * parts * depth * (rows + 2 * WIDE),
            transcendentals=2 * rows * WIDE,
        ),
    )(own, gain, meta, *xs, *dep, *weights)


def across(value, turn):
    count = lax.axis_size("section")
    pairs = [(i, i ^ 1) if turn == 0 else (i, count - 1 - i) for i in range(count)]
    return lax.ppermute(value, "section", pairs)


def to_all(value, axis):
    count = lax.axis_size(axis)
    return lax.all_to_all(jnp.broadcast_to(value[None], (count,) + value.shape), axis, 0, 0)


def shards(
    features,
    dw_weight,
    ln_gain,
    ln_bias,
    layer_scale,
    proj_weight,
    text_embed,
    positions,
    rms_gain,
    head_weight,
    labels,
):
    sections = lax.axis_size("section")
    parts = lax.axis_size("dp")
    shard_index = lax.axis_index(("section",) + VOCAB)
    places = positions[0]
    targets = labels[0]
    columns = head_weight.shape[1]
    slots = lax.iota(jnp.int32, targets.shape[0])

    text = to_all(text_embed[0], "section").reshape(slots.shape[0], -1)

    weight = head_weight.T
    low_all = lax.all_gather(weight[:LOW], "dp", axis=0)
    high = jnp.pad(weight[LOW:], ((0, 2 * WIDE - columns), (0, 0)))
    left, right = shifted(high, "dp", -1), shifted(high, "dp", 1)

    image = features[0]
    height, width, chans = image.shape
    padded = extended(image, VOCAB, 3)
    padded = jnp.pad(padded, ((0, 0), (3, 3), (0, 0))).astype(jnp.float32)
    conv = jnp.zeros((height, width, chans), jnp.float32)
    for row_off in range(7):
        for col_off in range(7):
            conv = (
                conv
                + padded[row_off : row_off + height, col_off : col_off + width]
                * dw_weight[row_off, col_off]
            )
    sums = jnp.stack(
        [jnp.sum(conv, axis=-1).reshape(-1), jnp.sum(conv * conv, axis=-1).reshape(-1)]
    )
    sums = lax.psum(sums, "section")

    is_text = jnp.all(slots[:, None] != places[None, :], axis=1)
    rank = jnp.sum(
        jnp.where((slots[None, :] < slots[:, None]) & is_text[None, :], 1, 0), axis=1
    )
    text_rows = slots.shape[0] - places.shape[0]
    select = (rank[None, :] == lax.iota(jnp.int32, text_rows)[:, None]) & is_text[None, :]
    text, _, _ = lax.optimization_barrier((text, sums, low_all))
    text = jnp.dot(
        select.astype(jnp.bfloat16), text, preferred_element_type=jnp.float32
    ).astype(jnp.bfloat16)
    text_slots = jnp.sum(jnp.where(select, slots[None, :], 0), axis=1)
    text_all = lax.all_gather(text, VOCAB, axis=0)
    text_all = text_all.reshape(tuple(lax.axis_size(axis) for axis in VOCAB) + text.shape)
    all_chans = chans * sections
    middle = sums[0].reshape(height, width) / all_chans
    spread = sums[1].reshape(height, width) / all_chans - middle * middle
    normal = (conv - middle[..., None]) * lax.rsqrt(spread + 1e-06)[..., None] * ln_gain + ln_bias
    block = image.astype(jnp.float32) + layer_scale * normal
    pooled = block.reshape(height // 4, 4, width // 4, 4, chans).mean(axis=(1, 3))
    pooled = pooled.reshape(-1, chans).astype(jnp.bfloat16)

    tokens = to_all(pooled, VOCAB).reshape(-1, chans)
    rows = jnp.dot(tokens, proj_weight, preferred_element_type=jnp.float32)
    for turn in range(2):
        rows = rows + across(rows.astype(jnp.bfloat16), turn).astype(jnp.float32)
    rows = rows.astype(jnp.bfloat16)

    rows, left, right = lax.optimization_barrier((rows, left, right))
    half = high.shape[0] // 2
    far, off = shifted(left[:half], "dp", -1), shifted(right[half:], "dp", 1)
    rows = to_all(rows, "zl")
    rows, text_all = lax.optimization_barrier((rows, text_all))
    early = rows
    rows = to_all(rows, "y")
    rows, far, off, low_all = lax.optimization_barrier((rows, far, off, low_all))
    partner = lax.ppermute(rows, "core", [(0, 1), (1, 0)])

    gain = rms_gain.reshape(-1, 1, text.shape[1])
    own = jnp.stack([lax.axis_index("dp"), lax.axis_index("core")])
    offsets = (0, parts - 1, 1, 2)

    def stats(at, xs, dep):
        ids = jnp.sum(jnp.where(at[:, None] == slots[None, :], targets[None, :], 0), axis=1)
        ids = ids - shard_index * columns
        return head_stats(
            own,
            gain,
            jnp.stack([at, ids], axis=1),
            xs,
            (low_all, high, left, right, far, off),
            dep,
            columns,
            offsets,
            targets.shape[0],
        )

    of_text = stats(text_slots, (text_all,), (early,))
    of_visual = stats(places, (rows, partner), ())
    both = (of_text + of_visual)[:3]

    def merged(pieces):
        tops, totals, chosen = pieces[:, 0], pieces[:, 1], pieces[:, 2]
        top = jnp.max(tops, axis=0)
        return jnp.stack(
            [top, jnp.sum(totals * jnp.exp(tops - top), axis=0), jnp.sum(chosen, axis=0)]
        )

    for turn in range(2):
        both = merged(jnp.stack([both, across(both, turn)]))
    both = both.reshape(3, sections, -1)
    both = lax.dynamic_index_in_dim(both, lax.axis_index("section"), 1, keepdims=False)
    top, total, chosen = merged(to_all(both, VOCAB))
    loss = top + jnp.log(total) - chosen
    return (pooled[None], loss[None])


def solution(mesh):
    in_specs = (
        P("dp", VOCAB, None, "section"),
        P(None, None, "section"),
        P("section"),
        P("section"),
        P("section"),
        P("section", VOCAB),
        P("dp", "section", VOCAB),
        P("dp", None),
        P(),
        P("dp", ("section",) + VOCAB),
        P("dp", None),
    )
    out_specs = (P("dp", VOCAB, "section"), P("dp", "section"))
    sizes = (mesh.shape["section"], mesh.shape["vocab"] // 8, 4, 2, mesh.shape["dp"])
    mesh = jax.sharding.Mesh(mesh.devices.reshape(sizes), ("section",) + VOCAB + ("dp",))
    return jax.shard_map(shards, mesh=mesh, in_specs=in_specs, out_specs=out_specs, check_vma=False)
```
